128 devices in a mesh: seq: 32 (over x, y, core), head: 4 (over z).
Axes of the slice: x: 4, y: 4, z: 4, core: 2. Of those that a mesh axis runs over, the one named last changes fastest.
Arguments:
- query_rows: bfloat16 [16384, 64, 128], P('seq', 'head'), may hold values from -3 to 3
- key_rows: bfloat16 [16384, 64, 128], P('seq', 'head'), may hold values from -0.59765625 to 0.59765625
- value_rows: bfloat16 [16384, 64, 128], P('seq', 'head'), may hold values from -18 to 18
- output_grad: bfloat16 [16384, 64, 128], P('seq', 'head'), may hold values from -1.796875 to 1.796875
- norm_gain: float32 [64, 128], P('head'), may hold values from 0.1 to 1.9
- log_decay: float32 [64, 16384], P('head', 'seq'), may hold values from -0.6932 to 0, as said below
Outputs:
- normed: bfloat16 [16384, 64, 128], P('seq', 'head')
- grad_q: bfloat16 [16384, 64, 128], P('seq', 'head')
- grad_k: bfloat16 [16384, 64, 128], P('seq', 'head')
- grad_v: bfloat16 [16384, 64, 128], P('seq', 'head')
The draws below stay inside these ranges and needn't reach their ends.
Inputs may be any that keep to these rules, and one draw needn't show every extreme that they name: `log_decay`: never positive.
All inputs are finite; a program needn't handle non-finite values.
Results may differ from the reference program's by a relative error of at most 0.0051.
Values sent between devices are 32-bit elements; how exact they have to be, the bound alone decides.
A program may use at most 192 MiB of HBM per device.

```python
import jax
import jax.numpy as jnp
from jax import lax

HEAD_TOTAL = 64
HD = 128
BLOCK = 256
TOK_DEV = 512
TOKEN_TOTAL = 16384


def draw_log_decay(key, part):
    sequence_portions = jax.random.split(jax.random.fold_in(key, 11), 7)
    share = 0.5
    slow_mask = jax.random.uniform(sequence_portions[0], (HEAD_TOTAL, 1)) < share
    slow_rate = jnp.exp(jax.random.uniform(sequence_portions[1], (HEAD_TOTAL, 1), minval=jnp.log(0.02), maxval=jnp.log(0.5))) / TOKEN_TOTAL
    fast_rate = jnp.exp(jax.random.uniform(sequence_portions[2], (HEAD_TOTAL, 1), minval=jnp.log(5.0), maxval=jnp.log(8.0))) / BLOCK
    baseline_decay_rate = jnp.where(slow_mask, slow_rate, fast_rate)
    portion_decay_factor = jax.random.uniform(sequence_portions[3], (HEAD_TOTAL, TOKEN_TOTAL // TOK_DEV, 1), minval=0.5, maxval=1.5)
    portion_decay_factor = jnp.broadcast_to(portion_decay_factor, (HEAD_TOTAL, TOKEN_TOTAL // TOK_DEV, TOK_DEV)).reshape(HEAD_TOTAL, TOKEN_TOTAL)
    coarse_decay_factor = jax.random.uniform(sequence_portions[4], (HEAD_TOTAL, TOKEN_TOTAL), minval=0.6, maxval=1.4)
    sudden_decay_mask = jax.random.uniform(sequence_portions[5], (HEAD_TOTAL, TOKEN_TOTAL)) < 2.0 / TOKEN_TOTAL
    sudden_decay_drop = jnp.log(jax.random.uniform(sequence_portions[6], (HEAD_TOTAL, TOKEN_TOTAL), minval=0.5, maxval=0.8))
    return jnp.where(sudden_decay_mask, sudden_decay_drop, -baseline_decay_rate * portion_decay_factor * coarse_decay_factor).astype(jnp.float32)


def draw_query_rows(key, part):
    sequence_portions = jax.random.split(jax.random.fold_in(key, 23), 2)
    row_scale = jnp.exp(jax.random.uniform(sequence_portions[0], (TOKEN_TOTAL, 1, 1), minval=0.0, maxval=jnp.log(10.0)))
    base = jnp.clip(jax.random.normal(sequence_portions[1], (TOKEN_TOTAL, HEAD_TOTAL, HD)), -6.0, 6.0)
    return (0.05 * row_scale * base).astype(jnp.bfloat16)


def draw_value_rows(key, part):
    sequence_portions = jax.random.split(jax.random.fold_in(key, 37), 2)
    ramp = jnp.arange(HEAD_TOTAL, dtype=jnp.float32)[None, :, None] / (HEAD_TOTAL - 1)
    head_scale = 0.3 * jnp.exp(ramp * jnp.log(10.0))
    base = jnp.clip(jax.random.normal(sequence_portions[1], (TOKEN_TOTAL, HEAD_TOTAL, HD)), -6.0, 6.0)
    return (head_scale * base).astype(jnp.bfloat16)


def shard_levels(stream_key, dims, pieces, low, top_value):
    def one(axis_at, blocks):
        steps = jax.random.uniform(jax.random.fold_in(jax.random.fold_in(stream_key, 6), axis_at), (blocks,), jnp.float32, low / len(pieces), top_value / len(pieces))
        return jnp.repeat(jnp.exp(steps), dims[axis_at] // blocks).reshape((-1,) + (1,) * (len(dims) - axis_at - 1))

    loudness = one(*pieces[0])
    for cut in pieces[1:]:
        loudness = loudness * one(*cut)
    return loudness


def scatter_about(rng, dims, deviation, bound, pieces=(), kind=jnp.bfloat16):
    entries = jax.random.normal(rng, dims, jnp.float32) * deviation
    if len(pieces) > 0:
        entries = shard_levels(rng, dims, pieces, -0.22, 0.18) * entries
    return jnp.clip(entries, min=-bound, max=bound).astype(kind)


def setup_inputs(seed: int = 0) -> dict:
    streams_of = jax.random.split(jax.random.key(seed), 7)
    return {
        "query_rows": draw_query_rows(jax.random.fold_in(streams_of[6], 71), 0),
        "key_rows": scatter_about(streams_of[1], (TOKEN_TOTAL, HEAD_TOTAL, HD), 0.1, 0.59765625, ((0, 32), (1, 4))),
        "value_rows": draw_value_rows(jax.random.fold_in(streams_of[6], 71), 0),
        "output_grad": scatter_about(streams_of[3], (TOKEN_TOTAL, HEAD_TOTAL, HD), 0.3, 1.796875, ((0, 32), (1, 4))),
        "norm_gain": jnp.clip(1.0 + 0.18 * jax.random.normal(streams_of[4], (HEAD_TOTAL, HD), jnp.float32), 0.1, 1.9),
        "log_decay": draw_log_decay(jax.random.fold_in(streams_of[6], 71), 0),
    }


state_precision = lax.Precision.HIGH

def decay_table(cum_block):
    block_len = cum_block.shape[1]
    lower_mask = jnp.arange(block_len)[:, None] >= jnp.arange(block_len)[None, :]
    gap_table = jnp.where(lower_mask[None], cum_block[:, :, None] - cum_block[:, None, :], -jnp.inf)
    return jnp.exp(gap_table)

def reference(query_rows, key_rows, value_rows, output_grad, norm_gain, log_decay):
    nblocks = TOKEN_TOTAL // BLOCK
    query_blocks = query_rows.reshape(nblocks, BLOCK, HEAD_TOTAL, HD)
    key_blocks = key_rows.reshape(nblocks, BLOCK, HEAD_TOTAL, HD)
    value_blocks = value_rows.reshape(nblocks, BLOCK, HEAD_TOTAL, HD)
    grad_blocks = output_grad.reshape(nblocks, BLOCK, HEAD_TOTAL, HD)
    cum_all = jnp.cumsum(log_decay.reshape(HEAD_TOTAL, nblocks, BLOCK), axis=2).transpose(1, 0, 2)

    def forward_step(state_now, items):
        query_block, key_block, value_block, cum_block, grad_block = items
        query_f = query_block.astype(jnp.float32)
        key_f = key_block.astype(jnp.float32)
        value_f = value_block.astype(jnp.float32)
        decay = decay_table(cum_block)
        raw_scores = jnp.einsum('thd,shd->hts', query_f, key_f, precision=state_precision)
        weights = (raw_scores * decay).astype(jnp.bfloat16)
        inner_part = jnp.einsum('hts,shd->thd', weights.astype(jnp.float32), value_f, precision=state_precision)
        start_scale = jnp.exp(cum_block).T[:, :, None]
        attended = inner_part + jnp.einsum('thd,hde->the', query_f * start_scale, state_now, precision=state_precision)
        last_cum = cum_block[:, -1]
        end_scale = jnp.exp(last_cum[:, None] - cum_block).T[:, :, None]
        state_next = jnp.exp(last_cum)[:, None, None] * state_now + jnp.einsum('shd,she->hde', key_f * end_scale, value_f, precision=state_precision)
        mean_sq = lax.optimization_barrier(jnp.mean(attended * attended, axis=(1, 2)))
        inv_rms = lax.rsqrt(mean_sq + 1e-06)
        hat_rows = attended * inv_rms[:, None, None]
        normed = (hat_rows * norm_gain).astype(jnp.bfloat16)
        scaled = norm_gain * grad_block.astype(jnp.float32)
        projection = lax.optimization_barrier(jnp.mean(scaled * hat_rows, axis=(1, 2)))
        grad_attn = ((scaled - hat_rows * projection[:, None, None]) * inv_rms[:, None, None]).astype(jnp.bfloat16)
        return (state_next, (normed, grad_attn, state_now))
    zero_state = jnp.zeros((HEAD_TOTAL, HD, HD), jnp.float32)
    unused, (normed_all, grad_attn_all, states_all) = lax.scan(forward_step, zero_state, (query_blocks, key_blocks, value_blocks, cum_all, grad_blocks))

    def backward_step(grad_state, items):
        query_block, key_block, value_block, cum_block, grad_block, state_now = items
        query_f = query_block.astype(jnp.float32)
        key_f = key_block.astype(jnp.float32)
        value_f = value_block.astype(jnp.float32)
        grad_f = grad_block.astype(jnp.float32)
        decay = decay_table(cum_block)
        raw_scores = jnp.einsum('thd,shd->hts', query_f, key_f, precision=state_precision)
        weights = (raw_scores * decay).astype(jnp.bfloat16).astype(jnp.float32)
        grad_scores = (jnp.einsum('the,she->hts', grad_f, value_f, precision=state_precision) * decay).astype(jnp.bfloat16).astype(jnp.float32)
        start_scale = jnp.exp(cum_block).T[:, :, None]
        last_cum = cum_block[:, -1]
        end_scale = jnp.exp(last_cum[:, None] - cum_block).T[:, :, None]
        grad_query = jnp.einsum('hts,shd->thd', grad_scores, key_f, precision=state_precision) + jnp.einsum('the,hde->thd', grad_f * start_scale, state_now, precision=state_precision)
        grad_key = jnp.einsum('hts,thd->shd', grad_scores, query_f, precision=state_precision) + jnp.einsum('she,hde->shd', value_f * end_scale, grad_state, precision=state_precision)
        grad_value = jnp.einsum('hts,the->she', weights, grad_f, precision=state_precision) + jnp.einsum('shd,hde->she', key_f * end_scale, grad_state, precision=state_precision)
        grad_prev = jnp.exp(last_cum)[:, None, None] * grad_state + jnp.einsum('thd,the->hde', query_f * start_scale, grad_f, precision=state_precision)
        return (grad_prev, (grad_query.astype(jnp.bfloat16), grad_key.astype(jnp.bfloat16), grad_value.astype(jnp.bfloat16)))
    unused_grad, (grad_q, grad_k, grad_v) = lax.scan(backward_step, zero_state, (query_blocks, key_blocks, value_blocks, cum_all, grad_attn_all, states_all), reverse=True)
    shape_out = (TOKEN_TOTAL, HEAD_TOTAL, HD)
    return (normed_all.reshape(shape_out), grad_q.reshape(shape_out), grad_k.reshape(shape_out), grad_v.reshape(shape_out))
```

```python
import functools

import jax
import jax.numpy as jnp
from jax import lax
from jax.experimental import pallas as pl
from jax.experimental.pallas import tpu as pltpu
from jax.sharding import PartitionSpec as P

HEAD_TOTAL = 64
HD = 128
BLOCK = 256
CHUNK = 64
PAD = 8
MESH = pl.DeviceIdType.MESH
F32 = jnp.float32
BF16 = jnp.bfloat16


def dot(a, b, ca, cb):
    return lax.dot_general(a, b, (((ca,), (cb,)), ((), ())), preferred_element_type=F32)


def split(x, axis):
    hi = x.astype(BF16)
    lo = (x - hi.astype(F32)).astype(BF16)
    return jnp.concatenate([hi, lo], axis=axis)


def twice(x):
    return jnp.concatenate([x, x], axis=1)


def kernel(
    chips,
    q_hbm,
    k_hbm,
    v_hbm,
    g_hbm,
    gain_ref,
    ld_ref,
    normed_hbm,
    gq_hbm,
    gk_hbm,
    gv_hbm,
    land,
    hm,
    cumr,
    colc,
    att,
    wts,
    gkp,
    gvp,
    s0,
    g1,
    ob,
    gains,
    tx,
    tp,
    tm,
    sb,
    rb,
    pb,
    pin,
    es,
    ee,
    zb,
    sqacc,
    pracc,
    in_sem,
    out_sem,
    p1s,
    p1r,
    a1s,
    a1r,
    a2s,
    a2r,
    p2s,
    p2r,
    zs,
    zr,
):
    heads, tok = ld_ref.shape
    half = heads // 2
    nblocks = tok // BLOCK
    zcount = HEAD_TOTAL // heads
    d = lax.axis_index("seq")
    z = lax.axis_index("head")
    c = d // 2
    core = d - 2 * c
    partner = (2 * c + 1 - core, z)
    KS, VS, QS, GS = 0, 1, 2, 3

    def chip_dev(chip):
        return (2 * chip + core, z)

    def load(slot, src):
        return pltpu.make_async_copy(src, land.at[slot], in_sem.at[slot])

    sources = (k_hbm, v_hbm, q_hbm, g_hbm)
    for slot in range(4):
        load(slot, sources[slot]).start()

    barrier = pltpu.get_barrier_semaphore()

    def greet(i, _):
        pl.semaphore_signal(
            barrier, inc=1, device_id=chip_dev(lax.rem(c + i, chips)), device_id_type=MESH
        )
        return 0

    lax.fori_loop(1, chips, greet, 0)
    pl.semaphore_signal(barrier, inc=1, device_id=partner, device_id_type=MESH)
    for i in range(1, zcount):
        pl.semaphore_signal(
            barrier, inc=1, device_id=(d, lax.rem(z + i, zcount)), device_id_type=MESH
        )

    cum = ld_ref[...]
    lane = lax.broadcasted_iota(jnp.int32, cum.shape, 1) % BLOCK
    step = 1
    while step < BLOCK:
        cum = cum + jnp.where(lane >= step, pltpu.roll(cum, step, 1), 0.0)
        step *= 2
    for h in range(heads):
        cumr[h] = jnp.broadcast_to(cum[h : h + 1, :], (8, tok))
        gains[h] = jnp.broadcast_to(gain_ref[h : h + 1, :], (8, HD))

    def columns(h, _):
        colc[h] = jnp.transpose(jnp.broadcast_to(cumr[h, 0:1, :], (HD, tok)))
        return 0

    lax.fori_loop(0, heads, columns, 0)

    def to_heads(slot):
        load(slot, sources[slot]).wait()

        def part(i, _):
            at = pl.ds(pl.multiple_of(i * CHUNK, CHUNK), CHUNK)
            hm[slot, :, at, :] = pltpu.einshape("thd->htd", land[slot, at])
            return 0

        lax.fori_loop(0, tok // CHUNK, part, 0)

    def store_rows(slot, src, dst):
        def part(i, _):
            at = pl.ds(pl.multiple_of(i * CHUNK, CHUNK), CHUNK)
            land[slot, at] = pltpu.einshape("htd->thd", src[:, at, :])
            pltpu.make_async_copy(land.at[slot, at], dst.at[at], out_sem.at[slot, i]).start()
            return 0

        lax.fori_loop(0, tok // CHUNK, part, 0)

    def store_wait(slot, dst):
        def part(i, _):
            at = pl.ds(pl.multiple_of(i * CHUNK, CHUNK), CHUNK)
            pltpu.make_async_copy(land.at[slot, at], dst.at[at], out_sem.at[slot, i]).wait()
            return 0

        lax.fori_loop(0, tok // CHUNK, part, 0)

    def rows(b):
        return slice(b * BLOCK, (b + 1) * BLOCK)

    def end_row(h, b):
        return colc[h, (b + 1) * BLOCK - 1 : (b + 1) * BLOCK, :]

    mask = lax.broadcasted_iota(jnp.int32, (BLOCK, BLOCK), 0) >= lax.broadcasted_iota(
        jnp.int32, (BLOCK, BLOCK), 1
    )

    def decay_table(h, b):
        gap = twice(colc[h, rows(b), :]) - cumr[h, 0:1, rows(b)]
        return jnp.exp(jnp.where(mask, gap, -jnp.inf))

    def pair1(w, j):
        return pltpu.make_async_remote_copy(
            tx.at[w, j],
            tp.at[w, j],
            p1s.at[w, j],
            p1r.at[w, j],
            device_id=partner,
            device_id_type=MESH,
        )

    def spread1(w, dest, src):
        return pltpu.make_async_remote_copy(
            sb.at[w, dest],
            rb.at[w, src],
            a1s.at[w, dest],
            a1r.at[w, src],
            device_id=chip_dev(dest),
            device_id_type=MESH,
        )

    def spread2(w, dest, src):
        return pltpu.make_async_remote_copy(
            pb.at[w, dest],
            pin.at[w, src],
            a2s.at[w, dest],
            a2r.at[w, src],
            device_id=chip_dev(dest),
            device_id_type=MESH,
        )

    def pair2(w, j, owner):
        return pltpu.make_async_remote_copy(
            es.at[w, j],
            ee.at[w, owner * half + j],
            p2s.at[w, j],
            p2r.at[w, j],
            device_id=partner,
            device_id_type=MESH,
        )

    def begin(w, local_total):
        first = (core == 0) if w == 0 else (core == 1)

        def theirs(j, _):
            total, decay = local_total((1 - core) * half + j)
            tx[w, j, :HD] = total
            tx[w, j, HD:] = jnp.broadcast_to(decay, (PAD, HD))
            pair1(w, j).start()
            return 0

        lax.fori_loop(0, half, theirs, 0)

        def ours(i, _):
            j = lax.rem(i + c // 2, half)
            total, decay = local_total(core * half + j)
            tm[w, j, :HD] = total
            tm[w, j, HD:] = jnp.broadcast_to(decay, (PAD, HD))
            pair1(w, j).wait_recv()
            other = tp[w, j, :HD]
            other_decay = tp[w, j, HD : HD + 1]
            chip_total = jnp.where(first, other_decay, 1.0) * total + jnp.where(first, 1.0, decay) * other
            chip_decay = jnp.broadcast_to(decay * other_decay, (PAD, HD))
            for part in range(2):
                dest = 2 * j + part
                piece = chip_total[part * (HD // 2) : (part + 1) * (HD // 2)]
                sb[w, dest, : HD // 2] = piece
                sb[w, dest, HD // 2 :] = chip_decay

                @pl.when(dest != c)
                def _():
                    spread1(w, dest, c).start()

                @pl.when(dest == c)
                def _():
                    rb[w, c, : HD // 2] = piece
                    rb[w, c, HD // 2 :] = chip_decay

            return 0

        lax.fori_loop(0, half, ours, 0)

    def middle(w):
        def wait(i, _):
            src = lax.rem(c + i, chips)
            spread1(w, src, src).wait_recv()
            return 0

        lax.fori_loop(1, chips, wait, 0)
        carried = jnp.zeros((HD // 2, HD), F32)
        for i in range(chips):
            src = i if w == 0 else chips - 1 - i
            pb[w, src] = carried
            carried = rb[w, src, HD // 2 : HD // 2 + 1] * carried + rb[w, src, : HD // 2]

        def send(i, _):
            spread2(w, lax.rem(c + i, chips), c).start()
            return 0

        lax.fori_loop(1, chips, send, 0)
        pin[w, c] = pb[w, c]

    def finish(w, use):
        first = (core == 0) if w == 0 else (core == 1)

        def ours(i, _):
            j = lax.rem(i + c // 2, half)
            for part in range(2):
                src = 2 * j + part

                @pl.when(src != c)
                def _():
                    spread2(w, src, src).wait_recv()

            entering = jnp.concatenate([pin[w, 2 * j], pin[w, 2 * j + 1]], axis=0)
            decay = jnp.where(first, tm[w, j, HD : HD + 1], tp[w, j, HD : HD + 1])
            total = jnp.where(first, tm[w, j, :HD], tp[w, j, :HD])
            after = decay * entering + total
            es[w, j] = jnp.where(first, after, entering)
            pair2(w, j, core).start()
            ee[w, core * half + j] = jnp.where(first, entering, after)
            return 0

        lax.fori_loop(0, half, ours, 0)

        def use_ours(j, _):
            use(core * half + j)
            return 0

        lax.fori_loop(0, half, use_ours, 0)

        def use_theirs(i, _):
            j = lax.rem(i + c // 2, half)
            pair2(w, j, 1 - core).wait_recv()
            use((1 - core) * half + j)
            return 0

        lax.fori_loop(0, half, use_theirs, 0)

    def drain(w):
        def pairs(j, _):
            pair1(w, j).wait_send()
            pair2(w, j, core).wait_send()
            return 0

        lax.fori_loop(0, half, pairs, 0)

        def spreads(i, _):
            dest = lax.rem(c + i, chips)
            spread1(w, dest, c).wait_send()
            spread2(w, dest, c).wait_send()
            return 0

        lax.fori_loop(1, chips, spreads, 0)

    to_heads(KS)
    to_heads(VS)

    def key_value(h):
        parts = []
        for b in range(nblocks):
            scale = jnp.exp(end_row(h, b) - colc[h, rows(b), :])
            scaled = split(hm[VS, h, rows(b), :].astype(F32) * scale, 1)
            both = dot(hm[KS, h, rows(b), :], scaled, 0, 0)
            parts.append(both[:, :HD] + both[:, HD:])
        s0[h] = parts[0]
        return (
            jnp.exp(end_row(h, 1)) * parts[0] + parts[1],
            jnp.exp(end_row(h, 0) + end_row(h, 1)),
        )

    pl.semaphore_wait(barrier, chips - 1 + 1 + zcount - 1)
    begin(0, key_value)
    to_heads(QS)

    def intra_forward(h, _):
        for b in range(nblocks):
            raw = dot(hm[QS, h, rows(b), :], hm[KS, h, rows(b), :], 1, 1)
            weights = (raw * decay_table(h, b)).astype(BF16)
            wts[h, b] = weights
            att[h, rows(b), :] = dot(weights, hm[VS, h, rows(b), :], 1, 0)
        return 0

    lax.fori_loop(0, half, intra_forward, 0)
    middle(0)
    lax.fori_loop(half, heads, intra_forward, 0)
    to_heads(GS)

    def states(h):
        enter = ee[0, h]
        return enter, jnp.exp(end_row(h, 0)) * enter + s0[h]

    sqacc[...] = jnp.zeros_like(sqacc)
    pracc[...] = jnp.zeros_like(pracc)

    def attend(h):
        at_block = states(h)
        gain = gains[h, 0:1, :]
        for b in range(nblocks):
            carried = dot(twice(hm[QS, h, rows(b), :]), split(at_block[b], 0), 1, 0)
            whole = att[h, rows(b), :] + jnp.exp(colc[h, rows(b), :]) * carried
            att[h, rows(b), :] = whole
            sqacc[rows(b), :] += whole * whole
            pracc[rows(b), :] += (gain * hm[GS, h, rows(b), :].astype(F32)) * whole

    finish(0, attend)

    zb[0, 0:1, :] = jnp.sum(jnp.transpose(sqacc[...]), axis=0, keepdims=True)
    zb[0, 1:2, :] = jnp.sum(jnp.transpose(pracc[...]), axis=0, keepdims=True)
    zb[0, 2:, :] = jnp.zeros((6, tok), F32)

    def across(i):
        return pltpu.make_async_remote_copy(
            zb.at[0],
            zb.at[i],
            zs.at[i],
            zr.at[i],
            device_id=(d, lax.rem(z + i, zcount)),
            device_id_type=MESH,
        )

    for i in range(1, zcount):
        across(i).start()
    for i in range(1, zcount):
        across(i).wait()
    summed = zb[0]
    for i in range(1, zcount):
        summed = summed + zb[i]
    inv_row = lax.rsqrt(summed[0:1, :] / (HEAD_TOTAL * HD) + 1e-06)
    mean_row = summed[1:2, :] * inv_row / (HEAD_TOTAL * HD)
    sqacc[...] = jnp.transpose(jnp.broadcast_to(inv_row, (HD, tok)))
    pracc[...] = jnp.transpose(jnp.broadcast_to(inv_row * mean_row, (HD, tok)))

    def query_grad(h):
        gain = gains[h, 0:1, :]
        parts = []
        for b in range(nblocks):
            scaled = gain * hm[GS, h, rows(b), :].astype(F32)
            grad = ((scaled - att[h, rows(b), :] * pracc[rows(b), :]) * sqacc[rows(b), :]).astype(BF16)
            hm[GS, h, rows(b), :] = grad
            lifted = split(grad.astype(F32) * jnp.exp(colc[h, rows(b), :]), 1)
            both = dot(hm[QS, h, rows(b), :], lifted, 0, 0)
            parts.append(both[:, :HD] + both[:, HD:])
        g1[h] = parts[1]
        return (
            parts[0] + jnp.exp(end_row(h, 0)) * parts[1],
            jnp.exp(end_row(h, 0) + end_row(h, 1)),
        )

    begin(1, query_grad)

    def intra_backward(h, _):
        at_block = states(h)
        gain = gains[h, 0:1, :]
        for b in range(nblocks):
            ob[0, h, rows(b), :] = (att[h, rows(b), :] * sqacc[rows(b), :] * gain).astype(BF16)
            grad = hm[GS, h, rows(b), :]
            scores = (dot(grad, hm[VS, h, rows(b), :], 1, 1) * decay_table(h, b)).astype(BF16)
            carried = dot(twice(grad), split(at_block[b], 1), 1, 1)
            ob[1, h, rows(b), :] = (
                dot(scores, hm[KS, h, rows(b), :], 1, 0) + jnp.exp(colc[h, rows(b), :]) * carried
            ).astype(BF16)
            gkp[h, rows(b), :] = dot(scores, hm[QS, h, rows(b), :], 0, 0)
            gvp[h, rows(b), :] = dot(wts[h, b], grad, 0, 0)
        return 0

    lax.fori_loop(0, half, intra_backward, 0)
    middle(1)
    lax.fori_loop(half, heads, intra_backward, 0)
    store_rows(0, ob.at[0], normed_hbm)
    store_rows(1, ob.at[1], gq_hbm)

    def close(h):
        last = ee[1, h]
        at_block = (jnp.exp(end_row(h, 1)) * last + g1[h], last)
        for b in range(nblocks):
            scale = jnp.exp(end_row(h, b) - colc[h, rows(b), :])
            key = hm[KS, h, rows(b), :]
            value = hm[VS, h, rows(b), :]
            grad_k = gkp[h, rows(b), :] + scale * dot(twice(value), split(at_block[b], 1), 1, 1)
            grad_v = gvp[h, rows(b), :] + scale * dot(twice(key), split(at_block[b], 0), 1, 0)
            hm[KS, h, rows(b), :] = grad_k.astype(BF16)
            hm[VS, h, rows(b), :] = grad_v.astype(BF16)

    finish(1, close)
    store_rows(2, hm.at[KS], gk_hbm)
    store_rows(3, hm.at[VS], gv_hbm)
    drain(0)
    drain(1)
    for slot, dst in enumerate((normed_hbm, gq_hbm, gk_hbm, gv_hbm)):
        store_wait(slot, dst)


def on_device(chips, query_rows, key_rows, value_rows, output_grad, norm_gain, log_decay):
    tok, heads, _ = query_rows.shape
    half = heads // 2
    rows = jax.ShapeDtypeStruct((tok, heads, HD), BF16)
    hbm = pl.BlockSpec(memory_space=pl.ANY)
    vmem = pl.BlockSpec(memory_space=pltpu.VMEM)
    by_head = pltpu.VMEM((heads, tok, HD), F32)
    state = pltpu.VMEM((heads, HD, HD), F32)
    dma = pltpu.SemaphoreType.DMA
    return pl.pallas_call(
        functools.partial(kernel, chips),
        out_shape=(rows,) * 4,
        in_specs=[hbm] * 4 + [vmem] * 2,
        out_specs=[hbm] * 4,
        scratch_shapes=[
            pltpu.VMEM((4, tok, heads, HD), BF16),
            pltpu.VMEM((4, heads, tok, HD), BF16),
            pltpu.VMEM((heads, 8, tok), F32),
            by_head,
            by_head,
            pltpu.VMEM((heads, tok // BLOCK, BLOCK, BLOCK), BF16),
            by_head,
            by_head,
            state,
            state,
            pltpu.VMEM((2, heads, tok, HD), BF16),
            pltpu.VMEM((heads, 8, HD), F32),
            pltpu.VMEM((2, half, HD + PAD, HD), F32),
            pltpu.VMEM((2, half, HD + PAD, HD), F32),
            pltpu.VMEM((2, half, HD + PAD, HD), F32),
            pltpu.VMEM((2, chips, HD // 2 + PAD, HD), F32),
            pltpu.VMEM((2, chips, HD // 2 + PAD, HD), F32),
            pltpu.VMEM((2, chips, HD // 2, HD), F32),
            pltpu.VMEM((2, chips, HD // 2, HD), F32),
            pltpu.VMEM((2, half, HD, HD), F32),
            pltpu.VMEM((2, heads, HD, HD), F32),
            pltpu.VMEM((HEAD_TOTAL // heads, 8, tok), F32),
            pltpu.VMEM((tok, HD), F32),
            pltpu.VMEM((tok, HD), F32),
            dma((4,)),
            dma((4, tok // CHUNK)),
            dma((2, half)),
            dma((2, half)),
            dma((2, chips)),
            dma((2, chips)),
            dma((2, chips)),
            dma((2, chips)),
            dma((2, half)),
            dma((2, half)),
            dma((HEAD_TOTAL // heads,)),
            dma((HEAD_TOTAL // heads,)),
        ],
        compiler_params=pltpu.CompilerParams(
            collective_id=0, has_side_effects=True, vmem_limit_bytes=60 << 20
        ),
        cost_estimate=pl.CostEstimate(
            flops=2 * 10**10, bytes_accessed=16 << 20, transcendentals=10**7
        ),
    )(query_rows, key_rows, value_rows, output_grad, norm_gain, log_decay)


def solution(mesh):
    rows = P("seq", "head", None)
    return jax.shard_map(
        functools.partial(on_device, mesh.shape["seq"] // 2),
        mesh=mesh,
        in_specs=(rows, rows, rows, rows, P("head", None), P("head", "seq")),
        out_specs=(rows,) * 4,
        check_vma=False,
    )
```

```python
import functools

import jax
import jax.numpy as jnp
from jax import lax
from jax.experimental import pallas as pl
from jax.experimental.pallas import tpu as pltpu
from jax.sharding import PartitionSpec as P

HEAD_TOTAL = 64
HD = 128
BLOCK = 256
CHUNK = 64
PAD = 8
FIRST_VMEM = 38 << 20
SECOND_VMEM = 14 << 20
MESH = pl.DeviceIdType.MESH
F32 = jnp.float32
BF16 = jnp.bfloat16


def dot(a, b, ca, cb):
    return lax.dot_general(a, b, (((ca,), (cb,)), ((), ())), preferred_element_type=F32)


def split(x, axis):
    hi = x.astype(BF16)
    lo = (x - hi.astype(F32)).astype(BF16)
    return jnp.concatenate([hi, lo], axis=axis)


def twice(x):
    return jnp.concatenate([x, x], axis=1)


def one_device_ids(chips):
    d = lax.axis_index("seq")
    c = d // 2
    return d, c, d - 2 * c


def block_rows(b):
    return slice(b * BLOCK, (b + 1) * BLOCK)


def close_heads(hs, state, gkp, gvp, colc, keys, values, put):
    tok = colc.shape[1]
    for b in range(tok // BLOCK):
        rows = block_rows(b)
        loaded = []
        for h in hs:
            gap = colc[h, tok - 1 : tok, :] - colc[h, rows, :]
            for later in range(b, tok // BLOCK - 1):
                gap = gap + colc[h, (later + 1) * BLOCK - 1 : (later + 1) * BLOCK, :]
            loaded.append(
                (jnp.exp(gap), keys[h, rows, :], values[h, rows, :], state[h], gkp[h, rows, :], gvp[h, rows, :])
            )
        done = []
        for scale, key, value, last, part_k, part_v in loaded:
            grad_k = part_k + scale * dot(twice(value), split(last, 1), 1, 1)
            grad_v = part_v + scale * dot(twice(key), split(last, 0), 1, 0)
            done.append((grad_k.astype(BF16), grad_v.astype(BF16)))
        for h, (grad_k, grad_v) in zip(hs, done):
            put(h, rows, grad_k, grad_v)


def first_kernel(
    chips,
    q_hbm,
    k_hbm,
    v_hbm,
    g_hbm,
    gain_ref,
    ld_ref,
    normed_t,
    gq_t,
    gk_h,
    gv_h,
    gkp,
    gvp,
    enter_b,
    colc,
    land,
    qs,
    gs,
    cumr,
    att,
    wts,
    s0,
    g0,
    g1,
    ob,
    gains,
    tx,
    tp,
    tm,
    sb,
    rb,
    pb,
    pin,
    es,
    enter_f,
    zb,
    sqacc,
    pracc,
    in_sem,
    p1s,
    p1r,
    a1s,
    a1r,
    a2s,
    a2r,
    p2s,
    p2r,
    zs,
    zr,
):
    heads, tok = ld_ref.shape
    half = heads // 2
    pairs = half // 2
    zcount = HEAD_TOTAL // heads
    z = lax.axis_index("head")
    d, c, core = one_device_ids(chips)
    partner = (2 * c + 1 - core, z)
    ks, vs = gk_h, gv_h
    enter = (enter_f, enter_b)

    def chip_dev(chip):
        return (2 * chip + core, z)

    sources = (k_hbm, v_hbm, q_hbm, g_hbm)
    by_heads = (ks, vs, qs, gs)

    def load(slot):
        return pltpu.make_async_copy(sources[slot], land.at[slot % 3], in_sem.at[slot])

    for slot in range(3):
        load(slot).start()

    barrier = pltpu.get_barrier_semaphore()

    def greet(i, _):
        pl.semaphore_signal(
            barrier, inc=1, device_id=chip_dev(lax.rem(c + i, chips)), device_id_type=MESH
        )
        return 0

    lax.fori_loop(1, chips, greet, 0)
    pl.semaphore_signal(barrier, inc=1, device_id=partner, device_id_type=MESH)
    for i in range(1, zcount):
        pl.semaphore_signal(
            barrier, inc=1, device_id=(d, lax.rem(z + i, zcount)), device_id_type=MESH
        )

    cum = ld_ref[...]
    lane = lax.broadcasted_iota(jnp.int32, cum.shape, 1) % BLOCK
    step = 1
    while step < BLOCK:
        cum = cum + jnp.where(lane >= step, pltpu.roll(cum, step, 1), 0.0)
        step *= 2
    for h in range(heads):
        cumr[h] = jnp.broadcast_to(cum[h : h + 1, :], (8, tok))
        gains[h] = jnp.broadcast_to(gain_ref[h : h + 1, :], (8, HD))

    def columns(h, _):
        colc[h] = jnp.transpose(jnp.broadcast_to(cumr[h, 0:1, :], (HD, tok)))
        return 0

    lax.fori_loop(0, heads, columns, 0)

    def to_heads(slot):
        load(slot).wait()

        def part(i, _):
            at = pl.ds(pl.multiple_of(i * CHUNK, CHUNK), CHUNK)
            by_heads[slot][:, at, :] = pltpu.einshape("thd->htd", land[slot % 3, at])
            return 0

        lax.fori_loop(0, tok // CHUNK, part, 0)

    def to_rows(src, dst):
        def part(i, _):
            at = pl.ds(pl.multiple_of(i * CHUNK, CHUNK), CHUNK)
            dst[at] = pltpu.einshape("htd->thd", src[:, at, :])
            return 0

        lax.fori_loop(0, tok // CHUNK, part, 0)

    def end_row(h, b):
        return colc[h, (b + 1) * BLOCK - 1 : (b + 1) * BLOCK, :]

    mask = lax.broadcasted_iota(jnp.int32, (BLOCK, BLOCK), 0) >= lax.broadcasted_iota(
        jnp.int32, (BLOCK, BLOCK), 1
    )

    def decay_table(h, b):
        gap = twice(colc[h, block_rows(b), :]) - cumr[h, 0:1, block_rows(b)]
        return jnp.exp(jnp.where(mask, gap, -jnp.inf))

    def pair1(w, j):
        return pltpu.make_async_remote_copy(
            tx.at[w, j],
            tp.at[w, j],
            p1s.at[w, j],
            p1r.at[w, j],
            device_id=partner,
            device_id_type=MESH,
        )

    def spread1(w, dest, src):
        return pltpu.make_async_remote_copy(
            sb.at[w, dest],
            rb.at[w, src],
            a1s.at[w, dest],
            a1r.at[w, src],
            device_id=chip_dev(dest),
            device_id_type=MESH,
        )

    def spread2(w, dest, src):
        return pltpu.make_async_remote_copy(
            pb.at[w, dest],
            pin.at[w, src],
            a2s.at[w, dest],
            a2r.at[w, src],
            device_id=chip_dev(dest),
            device_id_type=MESH,
        )

    def pair2(w, j, owner):
        return pltpu.make_async_remote_copy(
            es.at[w, j],
            enter[w].at[owner * half + j],
            p2s.at[w, j],
            p2r.at[w, j],
            device_id=partner,
            device_id_type=MESH,
        )

    def far_first(i):
        return lax.rem(c + 1 + lax.rem(i + 5, chips - 1), chips)

    def begin(w, local_totals):
        first = (core == 0) if w == 0 else (core == 1)

        def theirs(i, _):
            js = (2 * i, 2 * i + 1)
            for j, (total, decay) in zip(js, local_totals([(1 - core) * half + j for j in js])):
                tx[w, j, :HD] = total
                tx[w, j, HD:] = jnp.broadcast_to(decay, (PAD, HD))
                pair1(w, j).start()
            return 0

        lax.fori_loop(0, pairs, theirs, 0)

        def ours(i, _):
            pair = lax.rem(i + c // 4 + pairs // 2, pairs)
            js = (2 * pair, 2 * pair + 1)
            for j, (total, decay) in zip(js, local_totals([core * half + j for j in js])):
                tm[w, j, :HD] = total
                tm[w, j, HD:] = jnp.broadcast_to(decay, (PAD, HD))
                pair1(w, j).wait_recv()
                other = tp[w, j, :HD]
                other_decay = tp[w, j, HD : HD + 1]
                chip_total = (
                    jnp.where(first, other_decay, 1.0) * total + jnp.where(first, 1.0, decay) * other
                )
                chip_decay = jnp.broadcast_to(decay * other_decay, (PAD, HD))
                for part in range(2):
                    dest = 2 * j + part
                    piece = chip_total[part * (HD // 2) : (part + 1) * (HD // 2)]
                    sb[w, dest, : HD // 2] = piece
                    sb[w, dest, HD // 2 :] = chip_decay

                    @pl.when(dest != c)
                    def _():
                        spread1(w, dest, c).start()

            return 0

        lax.fori_loop(0, pairs, ours, 0)
        rb[w, c] = sb[w, c]

    def middle(w):
        def wait(i, _):
            src = lax.rem(c + i, chips)
            spread1(w, src, src).wait_recv()
            return 0

        lax.fori_loop(1, chips, wait, 0)
        carried = jnp.zeros((HD // 2, HD), F32)
        for i in range(chips):
            src = i if w == 0 else chips - 1 - i
            pb[w, src] = carried
            carried = rb[w, src, HD // 2 : HD // 2 + 1] * carried + rb[w, src, : HD // 2]

        def send(i, _):
            spread2(w, far_first(i), c).start()
            return 0

        lax.fori_loop(0, chips - 1, send, 0)
        pin[w, c] = pb[w, c]

    def finish(w):
        first = (core == 0) if w == 0 else (core == 1)

        def ours(i, _):
            j = lax.rem(i + c // 2, half)
            for part in range(2):
                src = 2 * j + part

                @pl.when(src != c)
                def _():
                    spread2(w, src, src).wait_recv()

            entering = jnp.concatenate([pin[w, 2 * j], pin[w, 2 * j + 1]], axis=0)
            decay = jnp.where(first, tm[w, j, HD : HD + 1], tp[w, j, HD : HD + 1])
            total = jnp.where(first, tm[w, j, :HD], tp[w, j, :HD])
            after = decay * entering + total
            es[w, j] = jnp.where(first, after, entering)
            pair2(w, j, core).start()
            enter[w][core * half + j] = jnp.where(first, entering, after)
            return 0

        lax.fori_loop(0, half, ours, 0)

    def drain(w):
        def by_pair(j, _):
            pair1(w, j).wait_send()
            pair2(w, j, core).wait_send()
            return 0

        lax.fori_loop(0, half, by_pair, 0)

        def spreads(i, _):
            dest = lax.rem(c + i, chips)
            spread1(w, dest, c).wait_send()
            spread2(w, dest, c).wait_send()
            return 0

        lax.fori_loop(1, chips, spreads, 0)

    to_heads(0)
    load(3).start()
    to_heads(1)

    def key_value(hs):
        loaded = [
            [
                (
                    ks[h, block_rows(b), :],
                    vs[h, block_rows(b), :].astype(F32),
                    jnp.exp(end_row(h, b) - colc[h, block_rows(b), :]),
                )
                for b in range(2)
            ]
            for h in hs
        ]
        ends = [(jnp.exp(end_row(h, 0)), jnp.exp(end_row(h, 1))) for h in hs]
        out = []
        for h, blocks, (end0, end1) in zip(hs, loaded, ends):
            parts = []
            for key, value, scale in blocks:
                both = dot(key, split(value * scale, 1), 0, 0)
                parts.append(both[:, :HD] + both[:, HD:])
            out.append((end1 * parts[0] + parts[1], end0 * end1, parts[0]))
        for h, (_, _, part) in zip(hs, out):
            s0[h] = part
        return [o[:2] for o in out]

    pl.semaphore_wait(barrier, chips - 1 + 1 + zcount - 1)
    begin(0, key_value)
    to_heads(2)

    def intra_forward(h, _):
        for b in range(2):
            rows = block_rows(b)
            query = qs[h, rows, :]
            raw = dot(query, ks[h, rows, :], 1, 1)
            weights = (raw * decay_table(h, b)).astype(BF16)
            wts[h, b] = weights
            inner = dot(weights, vs[h, rows, :], 1, 0)
            if b == 1:
                inner = inner + jnp.exp(colc[h, rows, :]) * dot(twice(query), split(s0[h], 0), 1, 0)
            att[h, rows, :] = inner
        return 0

    lax.fori_loop(0, half, intra_forward, 0)
    middle(0)
    lax.fori_loop(half, heads, intra_forward, 0)
    to_heads(3)
    sqacc[...] = jnp.zeros_like(sqacc)
    pracc[...] = jnp.zeros_like(pracc)

    def attend(hs, b):
        rows = block_rows(b)
        loaded = []
        for h in hs:
            gap = colc[h, rows, :] if b == 0 else colc[h, rows, :] + end_row(h, 0)
            loaded.append(
                (
                    qs[h, rows, :],
                    enter_f[h],
                    jnp.exp(gap),
                    att[h, rows, :],
                    gains[h, 0:1, :] * gs[h, rows, :].astype(F32),
                )
            )
        squares, products = sqacc[rows, :], pracc[rows, :]
        done = []
        for query, state, scale, inner, scaled in loaded:
            whole = inner + scale * dot(twice(query), split(state, 0), 1, 0)
            squares += whole * whole
            products += scaled * whole
            done.append(whole)
        for h, whole in zip(hs, done):
            att[h, rows, :] = whole
        sqacc[rows, :] = squares
        pracc[rows, :] = products

    def across(b, i):
        return pltpu.make_async_remote_copy(
            zb.at[b, 0],
            zb.at[b, i],
            zs.at[b, i],
            zr.at[b, i],
            device_id=(d, lax.rem(z + i, zcount)),
            device_id_type=MESH,
        )

    finish(0)
    for b in range(2):

        def attend_ours(i, _):
            attend([core * half + 2 * i, core * half + 2 * i + 1], b)
            return 0

        def attend_theirs(i, _):
            pair = lax.rem(i + c // 4, pairs)
            js = (2 * pair, 2 * pair + 1)
            if b == 0:
                for j in js:
                    pair2(0, j, 1 - core).wait_recv()
            attend([(1 - core) * half + j for j in js], b)
            return 0

        lax.fori_loop(0, pairs, attend_ours, 0)
        lax.fori_loop(0, pairs, attend_theirs, 0)
        rows = block_rows(b)
        zb[b, 0, 0:1, :] = jnp.sum(jnp.transpose(sqacc[rows, :]), axis=0, keepdims=True)
        zb[b, 0, 1:2, :] = jnp.sum(jnp.transpose(pracc[rows, :]), axis=0, keepdims=True)
        zb[b, 0, 2:, :] = jnp.zeros((6, BLOCK), F32)
        for i in range(1, zcount):
            across(b, i).start()

    def grads(hs, b):
        rows = block_rows(b)
        loaded = [
            (
                gains[h, 0:1, :] * gs[h, rows, :].astype(F32),
                att[h, rows, :],
                jnp.exp(colc[h, rows, :]),
                qs[h, rows, :],
            )
            for h in hs
        ]
        inv, shift = sqacc[rows, :], pracc[rows, :]
        out = []
        for scaled, whole, scale, query in loaded:
            grad = ((scaled - whole * shift) * inv).astype(BF16)
            both = dot(query, split(grad.astype(F32) * scale, 1), 0, 0)
            out.append((grad, both[:, :HD] + both[:, HD:]))
        for h, (grad, _) in zip(hs, out):
            gs[h, rows, :] = grad
        return [part for _, part in out]

    def norms(b):
        for i in range(1, zcount):
            across(b, i).wait()
        summed = zb[b, 0]
        for i in range(1, zcount):
            summed = summed + zb[b, i]
        inv_row = lax.rsqrt(summed[0:1, :] / (HEAD_TOTAL * HD) + 1e-06)
        mean_row = summed[1:2, :] * inv_row / (HEAD_TOTAL * HD)
        rows = block_rows(b)
        sqacc[rows, :] = jnp.transpose(jnp.broadcast_to(inv_row, (HD, BLOCK)))
        pracc[rows, :] = jnp.transpose(jnp.broadcast_to(inv_row * mean_row, (HD, BLOCK)))

    norms(0)

    def early_grads(i, _):
        hs = (2 * i, 2 * i + 1)
        for h, part in zip(hs, grads(hs, 0)):
            g0[h] = part
        return 0

    lax.fori_loop(0, heads // 2, early_grads, 0)
    norms(1)

    def late_grads(hs):
        early = [(g0[h], jnp.exp(end_row(h, 0)), jnp.exp(end_row(h, 1))) for h in hs]
        parts = grads(hs, 1)
        for h, part in zip(hs, parts):
            g1[h] = part
        return [(part0 + end0 * part1, end0 * end1) for (part0, end0, end1), part1 in zip(early, parts)]

    begin(1, late_grads)

    def intra_backward(h, _):
        enter_h = enter_f[h]
        at_block = (enter_h, jnp.exp(end_row(h, 0)) * enter_h + s0[h])
        gain = gains[h, 0:1, :]
        for b in range(2):
            rows = block_rows(b)
            ob[0, h, rows, :] = (att[h, rows, :] * sqacc[rows, :] * gain).astype(BF16)
            grad = gs[h, rows, :]
            key, value = ks[h, rows, :], vs[h, rows, :]
            scores = (dot(grad, value, 1, 1) * decay_table(h, b)).astype(BF16)
            carried = dot(twice(grad), split(at_block[b], 1), 1, 1)
            ob[1, h, rows, :] = (
                dot(scores, key, 1, 0) + jnp.exp(colc[h, rows, :]) * carried
            ).astype(BF16)
            part_k = dot(scores, qs[h, rows, :], 0, 0)
            part_v = dot(wts[h, b], grad, 0, 0)
            if b == 0:
                scale = jnp.exp(end_row(h, 0) - colc[h, rows, :])
                part_k = part_k + scale * dot(twice(value), split(g1[h], 1), 1, 1)
                part_v = part_v + scale * dot(twice(key), split(g1[h], 0), 1, 0)
            gkp[h, rows, :] = part_k
            gvp[h, rows, :] = part_v
        return 0

    lax.fori_loop(0, half, intra_backward, 0)
    middle(1)
    lax.fori_loop(half, heads, intra_backward, 0)
    to_rows(ob.at[0], normed_t)
    to_rows(ob.at[1], gq_t)
    finish(1)

    def put(h, rows, grad_k, grad_v):
        gk_h[h, rows, :] = grad_k
        gv_h[h, rows, :] = grad_v

    def close_ours(i, _):
        hs = [core * half + 2 * i, core * half + 2 * i + 1]
        close_heads(hs, enter_b, gkp, gvp, colc, ks, vs, put)
        return 0

    lax.fori_loop(0, pairs, close_ours, 0)

    def arrived(j, _):
        pair2(1, j, 1 - core).wait_recv()
        return 0

    lax.fori_loop(0, half, arrived, 0)
    drain(0)
    drain(1)


def second_kernel(
    normed_t,
    gq_t,
    gk_h,
    gv_h,
    gkp,
    gvp,
    enter_b,
    colc,
    normed_hbm,
    gq_hbm,
    gk_hbm,
    gv_hbm,
    done_k,
    done_v,
    land,
    first_sem,
    out_sem,
):
    heads, tok = colc.shape[0], colc.shape[1]
    half = heads // 2
    core = lax.rem(lax.axis_index("seq"), 2)
    ready = [
        pltpu.make_async_copy(src, dst, first_sem.at[i])
        for i, (src, dst) in enumerate(((normed_t, normed_hbm), (gq_t, gq_hbm)))
    ]
    for copy in ready:
        copy.start()

    def put(h, rows, grad_k, grad_v):
        done_k[h, rows, :] = grad_k
        done_v[h, rows, :] = grad_v

    def close_theirs(i, _):
        hs = [(1 - core) * half + 2 * i, (1 - core) * half + 2 * i + 1]
        close_heads(hs, enter_b, gkp, gvp, colc, gk_h, gv_h, put)
        for j in range(2):
            h = core * half + 2 * i + j
            done_k[h] = gk_h[h]
            done_v[h] = gv_h[h]
        return 0

    lax.fori_loop(0, half // 2, close_theirs, 0)
    outs = ((done_k, gk_hbm), (done_v, gv_hbm))

    def out(slot, i):
        at = pl.ds(pl.multiple_of(i * CHUNK, CHUNK), CHUNK)
        return pltpu.make_async_copy(land.at[slot, at], outs[slot][1].at[at], out_sem.at[slot, i])

    for slot in range(2):

        def part(i, _):
            at = pl.ds(pl.multiple_of(i * CHUNK, CHUNK), CHUNK)
            land[slot, at] = pltpu.einshape("htd->thd", outs[slot][0][:, at, :])
            out(slot, i).start()
            return 0

        lax.fori_loop(0, tok // CHUNK, part, 0)
    for slot in range(2):

        def wait(i, _):
            out(slot, i).wait()
            return 0

        lax.fori_loop(0, tok // CHUNK, wait, 0)
    for copy in ready:
        copy.wait()


def on_device(chips, query_rows, key_rows, value_rows, output_grad, norm_gain, log_decay):
    tok, heads, _ = query_rows.shape
    half = heads // 2
    zcount = HEAD_TOTAL // heads
    rows = jax.ShapeDtypeStruct((tok, heads, HD), BF16)
    hbm = pl.BlockSpec(memory_space=pl.ANY)
    vmem = pl.BlockSpec(memory_space=pltpu.VMEM)
    dma = pltpu.SemaphoreType.DMA

    def by_head(dtype):
        return pltpu.VMEM((heads, tok, HD), dtype)

    state = pltpu.VMEM((heads, HD, HD), F32)
    between = (
        pltpu.VMEM((tok, heads, HD), BF16),
        pltpu.VMEM((tok, heads, HD), BF16),
        by_head(BF16),
        by_head(BF16),
        by_head(F32),
        by_head(F32),
        state,
        by_head(F32),
    )
    made = pl.pallas_call(
        functools.partial(first_kernel, chips),
        out_shape=between,
        in_specs=[hbm] * 4 + [vmem] * 2,
        out_specs=[vmem] * len(between),
        scratch_shapes=[
            pltpu.VMEM((3, tok, heads, HD), BF16),
            by_head(BF16),
            by_head(BF16),
            pltpu.VMEM((heads, 8, tok), F32),
            by_head(F32),
            pltpu.VMEM((heads, tok // BLOCK, BLOCK, BLOCK), BF16),
            state,
            state,
            state,
            pltpu.VMEM((2, heads, tok, HD), BF16),
            pltpu.VMEM((heads, 8, HD), F32),
            pltpu.VMEM((2, half, HD + PAD, HD), F32),
            pltpu.VMEM((2, half, HD + PAD, HD), F32),
            pltpu.VMEM((2, half, HD + PAD, HD), F32),
            pltpu.VMEM((2, chips, HD // 2 + PAD, HD), F32),
            pltpu.VMEM((2, chips, HD // 2 + PAD, HD), F32),
            pltpu.VMEM((2, chips, HD // 2, HD), F32),
            pltpu.VMEM((2, chips, HD // 2, HD), F32),
            pltpu.VMEM((2, half, HD, HD), F32),
            state,
            pltpu.VMEM((2, zcount, 8, BLOCK), F32),
            pltpu.VMEM((tok, HD), F32),
            pltpu.VMEM((tok, HD), F32),
            dma((4,)),
            dma((2, half)),
            dma((2, half)),
            dma((2, chips)),
            dma((2, chips)),
            dma((2, chips)),
            dma((2, chips)),
            dma((2, half)),
            dma((2, half)),
            dma((2, zcount)),
            dma((2, zcount)),
        ],
        compiler_params=pltpu.CompilerParams(
            collective_id=0, has_side_effects=True, vmem_limit_bytes=FIRST_VMEM
        ),
        cost_estimate=pl.CostEstimate(
            flops=2 * 10**10, bytes_accessed=8 << 20, transcendentals=10**7
        ),
    )(query_rows, key_rows, value_rows, output_grad, norm_gain, log_decay)
    made = [pltpu.with_memory_space_constraint(m, pltpu.VMEM) for m in made]
    return pl.pallas_call(
        second_kernel,
        out_shape=(rows,) * 4,
        in_specs=[vmem] * len(between),
        out_specs=[hbm] * 4,
        scratch_shapes=[
            by_head(BF16),
            by_head(BF16),
            pltpu.VMEM((2, tok, heads, HD), BF16),
            dma((2,)),
            dma((2, tok // CHUNK)),
        ],
        compiler_params=pltpu.CompilerParams(vmem_limit_bytes=SECOND_VMEM),
        cost_estimate=pl.CostEstimate(
            flops=2 * 10**9, bytes_accessed=8 << 20, transcendentals=10**6
        ),
    )(*made)


def solution(mesh):
    rows = P("seq", "head", None)
    return jax.shard_map(
        functools.partial(on_device, mesh.shape["seq"] // 2),
        mesh=mesh,
        in_specs=(rows, rows, rows, rows, P("head", None), P("head", "seq")),
        out_specs=(rows,) * 4,
        check_vma=False,
    )
```

```python
import functools

import jax
import jax.numpy as jnp
from jax import lax
from jax.experimental import pallas as pl
from jax.experimental.pallas import tpu as pltpu
from jax.sharding import PartitionSpec as P

HEAD_TOTAL = 64
HD = 128
BLOCK = 256
CHUNK = 64
PAD = 8
EARLY = 6
FIRST_VMEM = 38 << 20
SECOND_VMEM = 14 << 20
MESH = pl.DeviceIdType.MESH
F32 = jnp.float32
BF16 = jnp.bfloat16


def dot(a, b, ca, cb):
    return lax.dot_general(a, b, (((ca,), (cb,)), ((), ())), preferred_element_type=F32)


def split(x, axis):
    hi = x.astype(BF16)
    lo = (x - hi.astype(F32)).astype(BF16)
    return jnp.concatenate([hi, lo], axis=axis)


def split3(x):
    hi = x.astype(BF16).astype(F32)
    mid = (x - hi).astype(BF16).astype(F32)
    lo = (x - hi - mid).astype(BF16).astype(F32)
    return jnp.concatenate([hi, mid, lo], axis=0)


def far_offsets(chips):
    side = int(chips**0.5)

    def hops(o):
        return sum(min(n, side - n) for n in divmod(o, side))

    return sorted(range(1, chips), key=lambda o: (-hops(o), o))


def twice(x):
    return jnp.concatenate([x, x], axis=1)


def one_device_ids(chips):
    d = lax.axis_index("seq")
    c = d // 2
    return d, c, d - 2 * c


def block_rows(b):
    return slice(b * BLOCK, (b + 1) * BLOCK)


def close_heads(hs, state, gkp, gvp, kcol, decs, keys, values, put):
    for b in range(2):
        rows = block_rows(b)
        loaded = []
        for h in hs:
            last = state[h] * decs[1, h, 0:1, :] if b == 0 else state[h]
            loaded.append(
                (kcol[h, rows, :], keys[h, rows, :], values[h, rows, :], last, gkp[h, rows, :], gvp[h, rows, :])
            )
        done = []
        for scale, key, value, last, part_k, part_v in loaded:
            grad_k = part_k + scale * dot(twice(value), split(last, 1), 1, 1)
            grad_v = part_v + scale * dot(twice(key), split(last, 0), 1, 0)
            done.append((grad_k.astype(BF16), grad_v.astype(BF16)))
        for h, (grad_k, grad_v) in zip(hs, done):
            put(h, rows, grad_k, grad_v)


def first_kernel(
    chips,
    q_hbm,
    k_hbm,
    v_hbm,
    g_hbm,
    gain_ref,
    ld_ref,
    normed_t,
    gq_t,
    gk_h,
    gv_h,
    gkp,
    gvp,
    enter_b,
    kcol,
    decs,
    land,
    qs,
    gs,
    cumr,
    colc,
    ecol,
    att,
    wts,
    s0,
    g0,
    g1,
    gains,
    tx,
    tp,
    tm,
    sb,
    rb,
    pb,
    pin,
    es,
    enter_f,
    zb,
    sqacc,
    pracc,
    in_sem,
    p1s,
    p1r,
    a1s,
    a1r,
    a2s,
    a2r,
    p2s,
    p2r,
    zs,
    zr,
):
    heads, tok = ld_ref.shape
    half = heads // 2
    pairs = half // 2
    zcount = HEAD_TOTAL // heads
    z = lax.axis_index("head")
    d, c, core = one_device_ids(chips)
    partner = (2 * c + 1 - core, z)
    ks, vs = gk_h, gv_h
    enter = (enter_f, enter_b)

    def chip_dev(chip):
        return (2 * chip + core, z)

    sources = (k_hbm, v_hbm, q_hbm, g_hbm)
    by_heads = (ks, vs, qs, gs)

    def load(slot):
        return pltpu.make_async_copy(sources[slot], land.at[slot % 2], in_sem.at[slot])

    for slot in range(2):
        load(slot).start()
    barrier = pltpu.get_barrier_semaphore()
    offsets = far_offsets(chips)
    for o in offsets:
        pl.semaphore_signal(
            barrier, inc=1, device_id=chip_dev(lax.rem(c + o, chips)), device_id_type=MESH
        )
    for i in range(1, zcount):
        pl.semaphore_signal(
            barrier, inc=1, device_id=(d, lax.rem(z + i, zcount)), device_id_type=MESH
        )
    pl.semaphore_signal(barrier, inc=1, device_id=partner, device_id_type=MESH)

    triangle = (
        lax.broadcasted_iota(jnp.int32, (BLOCK, BLOCK), 0)
        <= lax.broadcasted_iota(jnp.int32, (BLOCK, BLOCK), 1)
    ).astype(BF16)
    terms = split3(ld_ref[...]).astype(BF16)
    cums = []
    for b in range(2):
        summed = dot(terms[:, block_rows(b)], triangle, 1, 0)
        cums.append(summed[:heads] + summed[heads : 2 * heads] + summed[2 * heads :])
    ends = [cum[:, BLOCK - 1 :] for cum in cums]
    for b in range(2):
        decay = jnp.broadcast_to(jnp.exp(ends[b]), (heads, HD))
        for h in range(heads):
            decs[b, h] = jnp.broadcast_to(decay[h : h + 1, :], (8, HD))
    for h in range(heads):
        gains[h] = jnp.broadcast_to(gain_ref[h : h + 1, :], (8, HD))

    def columns(x, out):
        padded = jnp.concatenate([split3(x), jnp.zeros((HD - 3 * heads, tok), F32)], axis=0)
        upright = jnp.transpose(padded).astype(BF16)
        term_head = lax.broadcasted_iota(jnp.int32, (HD, 2 * HD), 0) % heads
        lane_head = lax.broadcasted_iota(jnp.int32, (HD, 2 * HD), 1) // HD

        for i in range(heads // 2):
            pick = (term_head == lane_head + 2 * i).astype(F32).astype(BF16)
            both = dot(upright, pick, 1, 0)
            out[2 * i] = both[:, :HD]
            out[2 * i + 1] = both[:, HD:]

    cum = jnp.concatenate(cums, axis=1)
    columns(jnp.concatenate([jnp.exp(e - x) for e, x in zip(ends, cums)], axis=1), kcol)

    def to_heads(slot):
        load(slot).wait()

        def part(i, _):
            at = pl.ds(pl.multiple_of(i * CHUNK, CHUNK), CHUNK)
            by_heads[slot][:, at, :] = pltpu.einshape("thd->htd", land[slot % 2, at])
            return 0

        lax.fori_loop(0, tok // CHUNK, part, 0)

    def to_rows(get, dst):
        def part(i, _):
            at = pl.ds(pl.multiple_of(i * CHUNK, CHUNK), CHUNK)
            dst[at] = pltpu.einshape("htd->thd", get(at))
            return 0

        lax.fori_loop(0, tok // CHUNK, part, 0)

    mask = lax.broadcasted_iota(jnp.int32, (BLOCK, BLOCK), 0) >= lax.broadcasted_iota(
        jnp.int32, (BLOCK, BLOCK), 1
    )

    def decay_table(h, b):
        gap = twice(colc[h, block_rows(b), :]) - cumr[h, 0:1, block_rows(b)]
        return jnp.exp(jnp.where(mask, gap, -jnp.inf))

    def pair1(w, j):
        return pltpu.make_async_remote_copy(
            tx.at[j],
            tp.at[w, j],
            p1s.at[w, j],
            p1r.at[w, j],
            device_id=partner,
            device_id_type=MESH,
        )

    def spread1(w, dest, src):
        return pltpu.make_async_remote_copy(
            sb.at[dest],
            rb.at[w, src],
            a1s.at[w, dest],
            a1r.at[w, src],
            device_id=chip_dev(dest),
            device_id_type=MESH,
        )

    def spread2(w, dest, src):
        return pltpu.make_async_remote_copy(
            pb.at[dest],
            pin.at[w, src],
            a2s.at[w, dest],
            a2r.at[w, src],
            device_id=chip_dev(dest),
            device_id_type=MESH,
        )

    def pair2(w, j, owner):
        return pltpu.make_async_remote_copy(
            es.at[j],
            enter[w].at[owner * half + j],
            p2s.at[w, j],
            p2r.at[w, j],
            device_id=partner,
            device_id_type=MESH,
        )

    def begin(w, local_totals):
        first = (core == 0) if w == 0 else (core == 1)

        def one(s, _):
            is_ours = jnp.logical_or(s == 2 * pairs - 1, jnp.logical_and(s >= 2, s % 2 == 0))
            i = jnp.where(is_ours, jnp.where(s == 2 * pairs - 1, pairs - 1, s // 2 - 1), (s + 1) // 2)
            pair = lax.rem(i + c // 4 + pairs // 2, pairs)
            js = (2 * pair, 2 * pair + 1)
            base = jnp.where(is_ours, core, 1 - core) * half
            totals = local_totals([base + j for j in js])
            if w == 0:

                @pl.when(s == 0)
                def _():
                    pl.semaphore_wait(barrier, chips - 1 + 1 + zcount - 1)

            @pl.when(jnp.logical_not(is_ours))
            def _():
                for j, (total, decay) in zip(js, totals):
                    tx[j, :HD] = total
                    tx[j, HD:] = jnp.broadcast_to(decay, (PAD, HD))
                    pair1(w, j).start()

            @pl.when(is_ours)
            def _():
                for j, (total, decay) in zip(js, totals):
                    tm[j, :HD] = total
                    tm[j, HD:] = jnp.broadcast_to(decay, (PAD, HD))
                    pair1(w, j).wait_recv()
                    other = tp[w, j, :HD]
                    other_decay = tp[w, j, HD : HD + 1]
                    chip_total = (
                        jnp.where(first, other_decay, 1.0) * total
                        + jnp.where(first, 1.0, decay) * other
                    )
                    chip_decay = jnp.broadcast_to(decay * other_decay, (PAD, HD))
                    for part in range(2):
                        dest = 2 * j + part
                        sb[dest, : HD // 2] = chip_total[part * (HD // 2) : (part + 1) * (HD // 2)]
                        sb[dest, HD // 2 :] = chip_decay

                        @pl.when(dest != c)
                        def _():
                            spread1(w, dest, c).start()

            return 0

        lax.fori_loop(0, 2 * pairs, one, 0)
        rb[w, c] = sb[c]

    def middle(w):
        for o in reversed(offsets):
            src = lax.rem(c + o, chips)
            spread1(w, src, src).wait_recv()
        carried = jnp.zeros((HD // 2, HD), F32)
        for i in range(chips):
            src = i if w == 0 else chips - 1 - i
            pb[src] = carried
            carried = rb[w, src, HD // 2 : HD // 2 + 1] * carried + rb[w, src, : HD // 2]

        for o in offsets:
            spread2(w, lax.rem(c + o, chips), c).start()
        pin[w, c] = pb[c]

    def finish(w):
        first = (core == 0) if w == 0 else (core == 1)

        def ours(i, _):
            j = lax.rem(i + c // 2, half)
            for part in range(2):
                src = 2 * j + part

                @pl.when(src != c)
                def _():
                    spread2(w, src, src).wait_recv()

            entering = jnp.concatenate([pin[w, 2 * j], pin[w, 2 * j + 1]], axis=0)
            decay = jnp.where(first, tm[j, HD : HD + 1], tp[w, j, HD : HD + 1])
            total = jnp.where(first, tm[j, :HD], tp[w, j, :HD])
            after = decay * entering + total
            es[j] = jnp.where(first, after, entering)
            pair2(w, j, core).start()
            enter[w][core * half + j] = jnp.where(first, entering, after)
            return 0

        lax.fori_loop(0, half, ours, 0)

    def drain(w):
        def by_pair(j, _):
            pair1(w, j).wait_send()
            pair2(w, j, core).wait_send()
            return 0

        lax.fori_loop(0, half, by_pair, 0)

        def spreads(i, _):
            dest = lax.rem(c + i, chips)
            spread1(w, dest, c).wait_send()
            spread2(w, dest, c).wait_send()
            return 0

        lax.fori_loop(1, chips, spreads, 0)

    to_heads(0)
    load(2).start()
    to_heads(1)
    load(3).start()

    def key_value(hs):
        loaded = [
            [
                (ks[h, block_rows(b), :], vs[h, block_rows(b), :].astype(F32), kcol[h, block_rows(b), :])
                for b in range(2)
            ]
            for h in hs
        ]
        decays = [(decs[0, h, 0:1, :], decs[1, h, 0:1, :]) for h in hs]
        out = []
        for blocks, (end0, end1) in zip(loaded, decays):
            parts = []
            for key, value, scale in blocks:
                both = dot(key, split(value * scale, 1), 0, 0)
                parts.append(both[:, :HD] + both[:, HD:])
            out.append((end1 * parts[0] + parts[1], end0 * end1, parts[0]))
        for h, (_, _, part) in zip(hs, out):
            s0[h] = part
        return [o[:2] for o in out]

    begin(0, key_value)
    for h in range(heads):
        cumr[h] = jnp.broadcast_to(cum[h : h + 1, :], (8, tok))
    columns(cum, colc)
    columns(jnp.exp(cum), ecol)
    to_heads(2)

    def intra_forward(h, _):
        for b in range(2):
            rows = block_rows(b)
            query = qs[h, rows, :]
            raw = dot(query, ks[h, rows, :], 1, 1)
            weights = (raw * decay_table(h, b)).astype(BF16)
            wts[h, b] = weights
            inner = dot(weights, vs[h, rows, :], 1, 0)
            if b == 1:
                inner = inner + ecol[h, rows, :] * dot(twice(query), split(s0[h], 0), 1, 0)
            att[h, rows, :] = inner
        return 0

    lax.fori_loop(0, EARLY, intra_forward, 0)
    middle(0)
    lax.fori_loop(EARLY, heads, intra_forward, 0)
    to_heads(3)
    sqacc[...] = jnp.zeros_like(sqacc)
    pracc[...] = jnp.zeros_like(pracc)

    def attend(hs, b):
        rows = block_rows(b)
        loaded = []
        for h in hs:
            state = enter_f[h] if b == 0 else enter_f[h] * decs[0, h, 0:1, :]
            loaded.append(
                (
                    qs[h, rows, :],
                    state,
                    ecol[h, rows, :],
                    att[h, rows, :],
                    gains[h, 0:1, :] * gs[h, rows, :].astype(F32),
                )
            )
        squares, products = sqacc[rows, :], pracc[rows, :]
        done = []
        for query, state, scale, inner, scaled in loaded:
            whole = inner + scale * dot(twice(query), split(state, 0), 1, 0)
            squares += whole * whole
            products += scaled * whole
            done.append(whole)
        for h, whole in zip(hs, done):
            att[h, rows, :] = whole
        sqacc[rows, :] = squares
        pracc[rows, :] = products

    def across(b, i):
        return pltpu.make_async_remote_copy(
            zb.at[b, 0],
            zb.at[b, i],
            zs.at[b, i],
            zr.at[b, i],
            device_id=(d, lax.rem(z + i, zcount)),
            device_id_type=MESH,
        )

    finish(0)
    for b in range(2):

        def attend_ours(i, _):
            attend([core * half + 4 * i + n for n in range(4)], b)
            return 0

        def attend_theirs(i, _):
            js = [4 * i + n for n in range(4)]
            if b == 0:
                for j in js:
                    pair2(0, j, 1 - core).wait_recv()
            attend([(1 - core) * half + j for j in js], b)
            return 0

        lax.fori_loop(0, pairs // 2, attend_ours, 0)
        lax.fori_loop(0, pairs // 2, attend_theirs, 0)
        rows = block_rows(b)
        zb[b, 0, 0:1, :] = jnp.sum(jnp.transpose(sqacc[rows, :]), axis=0, keepdims=True)
        zb[b, 0, 1:2, :] = jnp.sum(jnp.transpose(pracc[rows, :]), axis=0, keepdims=True)
        zb[b, 0, 2:, :] = jnp.zeros((6, BLOCK), F32)
        for i in range(1, zcount):
            across(b, i).start()

    def grads(hs, b):
        rows = block_rows(b)
        loaded = [
            (
                gains[h, 0:1, :] * gs[h, rows, :].astype(F32),
                att[h, rows, :],
                ecol[h, rows, :],
                qs[h, rows, :],
            )
            for h in hs
        ]
        inv, shift = sqacc[rows, :], pracc[rows, :]
        out = []
        for scaled, whole, scale, query in loaded:
            grad = ((scaled - whole * shift) * inv).astype(BF16)
            both = dot(query, split(grad.astype(F32) * scale, 1), 0, 0)
            out.append((grad, both[:, :HD] + both[:, HD:]))
        for h, (grad, _) in zip(hs, out):
            gs[h, rows, :] = grad
        return [part for _, part in out]

    def norms(b):
        for i in range(1, zcount):
            across(b, i).wait()
        summed = zb[b, 0]
        for i in range(1, zcount):
            summed = summed + zb[b, i]
        inv_row = lax.rsqrt(summed[0:1, :] / (HEAD_TOTAL * HD) + 1e-06)
        mean_row = summed[1:2, :] * inv_row / (HEAD_TOTAL * HD)
        rows = block_rows(b)
        sqacc[rows, :] = jnp.transpose(jnp.broadcast_to(inv_row, (HD, BLOCK)))
        pracc[rows, :] = jnp.transpose(jnp.broadcast_to(inv_row * mean_row, (HD, BLOCK)))

    norms(0)

    def early_grads(i, _):
        hs = [4 * i + n for n in range(4)]
        for h, part in zip(hs, grads(hs, 0)):
            g0[h] = part
        return 0

    lax.fori_loop(0, heads // 4, early_grads, 0)
    norms(1)

    def late_grads(hs):
        early = [(g0[h], decs[0, h, 0:1, :], decs[1, h, 0:1, :]) for h in hs]
        parts = grads(hs, 1)
        for h, part in zip(hs, parts):
            g1[h] = part
        return [(part0 + end0 * part1, end0 * end1) for (part0, end0, end1), part1 in zip(early, parts)]

    drain(0)
    begin(1, late_grads)

    def intra_backward(h, _):
        enter_h = enter_f[h]
        at_block = (enter_h, decs[0, h, 0:1, :] * enter_h + s0[h])
        for b in range(2):
            rows = block_rows(b)
            grad = gs[h, rows, :]
            key, value = ks[h, rows, :], vs[h, rows, :]
            scores = (dot(grad, value, 1, 1) * decay_table(h, b)).astype(BF16)
            carried = dot(twice(grad), split(at_block[b], 1), 1, 1)
            grad_q = dot(scores, key, 1, 0) + ecol[h, rows, :] * carried
            part_k = dot(scores, qs[h, rows, :], 0, 0)
            qs[h, rows, :] = grad_q.astype(BF16)
            part_v = dot(wts[h, b], grad, 0, 0)
            if b == 0:
                scale = kcol[h, rows, :]
                part_k = part_k + scale * dot(twice(value), split(g1[h], 1), 1, 1)
                part_v = part_v + scale * dot(twice(key), split(g1[h], 0), 1, 0)
            gkp[h, rows, :] = part_k
            gvp[h, rows, :] = part_v
        return 0

    lax.fori_loop(0, half, intra_backward, 0)
    middle(1)
    lax.fori_loop(half, heads, intra_backward, 0)

    def normed_part(at):
        gain = jnp.concatenate([gains[h, 0:1, :] for h in range(heads)], axis=0)
        return (att[:, at, :] * sqacc[at, :][None] * gain[:, None, :]).astype(BF16)

    to_rows(normed_part, normed_t)
    to_rows(lambda at: qs[:, at, :], gq_t)
    finish(1)

    def put(h, rows, grad_k, grad_v):
        gk_h[h, rows, :] = grad_k
        gv_h[h, rows, :] = grad_v

    def close_ours(i, _):
        hs = [core * half + 2 * i, core * half + 2 * i + 1]
        close_heads(hs, enter_b, gkp, gvp, kcol, decs, ks, vs, put)
        return 0

    lax.fori_loop(0, pairs, close_ours, 0)

    def arrived(j, _):
        pair2(1, j, 1 - core).wait_recv()
        return 0

    lax.fori_loop(0, half, arrived, 0)
    drain(1)


def second_kernel(
    normed_t,
    gq_t,
    gk_h,
    gv_h,
    gkp,
    gvp,
    enter_b,
    kcol,
    decs,
    normed_hbm,
    gq_hbm,
    gk_hbm,
    gv_hbm,
    done_k,
    done_v,
    land,
    first_sem,
    out_sem,
):
    heads, tok = kcol.shape[0], kcol.shape[1]
    half = heads // 2
    core = lax.rem(lax.axis_index("seq"), 2)
    ready = [
        pltpu.make_async_copy(src, dst, first_sem.at[i])
        for i, (src, dst) in enumerate(((normed_t, normed_hbm), (gq_t, gq_hbm)))
    ]
    for copy in ready:
        copy.start()

    def put(h, rows, grad_k, grad_v):
        done_k[h, rows, :] = grad_k
        done_v[h, rows, :] = grad_v

    def close_theirs(i, _):
        hs = [(1 - core) * half + 2 * i, (1 - core) * half + 2 * i + 1]
        close_heads(hs, enter_b, gkp, gvp, kcol, decs, gk_h, gv_h, put)
        for j in range(2):
            h = core * half + 2 * i + j
            done_k[h] = gk_h[h]
            done_v[h] = gv_h[h]
        return 0

    lax.fori_loop(0, half // 2, close_theirs, 0)
    outs = ((done_k, gk_hbm), (done_v, gv_hbm))

    def out(slot, i):
        at = pl.ds(pl.multiple_of(i * CHUNK, CHUNK), CHUNK)
        return pltpu.make_async_copy(land.at[slot, at], outs[slot][1].at[at], out_sem.at[slot, i])

    for slot in range(2):

        def part(i, _):
            at = pl.ds(pl.multiple_of(i * CHUNK, CHUNK), CHUNK)
            land[slot, at] = pltpu.einshape("htd->thd", outs[slot][0][:, at, :])
            out(slot, i).start()
            return 0

        lax.fori_loop(0, tok // CHUNK, part, 0)
    for slot in range(2):

        def wait(i, _):
            out(slot, i).wait()
            return 0

        lax.fori_loop(0, tok // CHUNK, wait, 0)
    for copy in ready:
        copy.wait()


def on_device(chips, query_rows, key_rows, value_rows, output_grad, norm_gain, log_decay):
    tok, heads, _ = query_rows.shape
    half = heads // 2
    zcount = HEAD_TOTAL // heads
    rows = jax.ShapeDtypeStruct((tok, heads, HD), BF16)
    hbm = pl.BlockSpec(memory_space=pl.ANY)
    vmem = pl.BlockSpec(memory_space=pltpu.VMEM)
    dma = pltpu.SemaphoreType.DMA

    def by_head(dtype):
        return pltpu.VMEM((heads, tok, HD), dtype)

    state = pltpu.VMEM((heads, HD, HD), F32)
    between = (
        pltpu.VMEM((tok, heads, HD), BF16),
        pltpu.VMEM((tok, heads, HD), BF16),
        by_head(BF16),
        by_head(BF16),
        by_head(F32),
        by_head(F32),
        state,
        by_head(F32),
        pltpu.VMEM((2, heads, 8, HD), F32),
    )
    made = pl.pallas_call(
        functools.partial(first_kernel, chips),
        out_shape=between,
        in_specs=[hbm] * 4 + [vmem] * 2,
        out_specs=[vmem] * len(between),
        scratch_shapes=[
            pltpu.VMEM((2, tok, heads, HD), BF16),
            by_head(BF16),
            by_head(BF16),
            pltpu.VMEM((heads, 8, tok), F32),
            by_head(F32),
            by_head(F32),
            by_head(F32),
            pltpu.VMEM((heads, tok // BLOCK, BLOCK, BLOCK), BF16),
            state,
            state,
            state,
            pltpu.VMEM((heads, 8, HD), F32),
            pltpu.VMEM((half, HD + PAD, HD), F32),
            pltpu.VMEM((2, half, HD + PAD, HD), F32),
            pltpu.VMEM((half, HD + PAD, HD), F32),
            pltpu.VMEM((chips, HD // 2 + PAD, HD), F32),
            pltpu.VMEM((2, chips, HD // 2 + PAD, HD), F32),
            pltpu.VMEM((chips, HD // 2, HD), F32),
            pltpu.VMEM((2, chips, HD // 2, HD), F32),
            pltpu.VMEM((half, HD, HD), F32),
            state,
            pltpu.VMEM((2, zcount, 8, BLOCK), F32),
            pltpu.VMEM((tok, HD), F32),
            pltpu.VMEM((tok, HD), F32),
            dma((4,)),
            dma((2, half)),
            dma((2, half)),
            dma((2, chips)),
            dma((2, chips)),
            dma((2, chips)),
            dma((2, chips)),
            dma((2, half)),
            dma((2, half)),
            dma((2, zcount)),
            dma((2, zcount)),
        ],
        compiler_params=pltpu.CompilerParams(
            collective_id=0, has_side_effects=True, vmem_limit_bytes=FIRST_VMEM
        ),
        cost_estimate=pl.CostEstimate(
            flops=2 * 10**10, bytes_accessed=8 << 20, transcendentals=10**7
        ),
    )(query_rows, key_rows, value_rows, output_grad, norm_gain, log_decay)
    made = [pltpu.with_memory_space_constraint(m, pltpu.VMEM) for m in made]
    return pl.pallas_call(
        second_kernel,
        out_shape=(rows,) * 4,
        in_specs=[vmem] * len(between),
        out_specs=[hbm] * 4,
        scratch_shapes=[
            by_head(BF16),
            by_head(BF16),
            pltpu.VMEM((2, tok, heads, HD), BF16),
            dma((2,)),
            dma((2, tok // CHUNK)),
        ],
        compiler_params=pltpu.CompilerParams(vmem_limit_bytes=SECOND_VMEM),
        cost_estimate=pl.CostEstimate(
            flops=2 * 10**9, bytes_accessed=8 << 20, transcendentals=10**6
        ),
    )(*made)


def solution(mesh):
    rows = P("seq", "head", None)
    return jax.shard_map(
        functools.partial(on_device, mesh.shape["seq"] // 2),
        mesh=mesh,
        in_specs=(rows, rows, rows, rows, P("head", None), P("head", "seq")),
        out_specs=(rows,) * 4,
        check_vma=False,
    )
```

```python
import functools

import jax
import jax.numpy as jnp
from jax import lax
from jax.experimental import pallas as pl
from jax.experimental.pallas import tpu as pltpu
from jax.sharding import PartitionSpec as P

HEAD_TOTAL = 64
HD = 128
BLOCK = 256
CHUNK = 64
PAD = 8
EARLY = 6
FIRST_VMEM = 38 << 20
SECOND_VMEM = 14 << 20
MESH = pl.DeviceIdType.MESH
F32 = jnp.float32
BF16 = jnp.bfloat16


def dot(a, b, ca, cb):
    return lax.dot_general(a, b, (((ca,), (cb,)), ((), ())), preferred_element_type=F32)


def split(x, axis):
    hi = x.astype(BF16)
    lo = (x - hi.astype(F32)).astype(BF16)
    return jnp.concatenate([hi, lo], axis=axis)


def split3(x):
    hi = x.astype(BF16).astype(F32)
    mid = (x - hi).astype(BF16).astype(F32)
    lo = (x - hi - mid).astype(BF16).astype(F32)
    return jnp.concatenate([hi, mid, lo], axis=0)


def far_offsets(chips):
    side = int(chips**0.5)

    def hops(o):
        return sum(min(n, side - n) for n in divmod(o, side))

    return sorted(range(1, chips), key=lambda o: (-hops(o), o))


def twice(x):
    return jnp.concatenate([x, x], axis=1)


def one_device_ids(chips):
    d = lax.axis_index("seq")
    c = d // 2
    return d, c, d - 2 * c


def block_rows(b):
    return slice(b * BLOCK, (b + 1) * BLOCK)


def close_heads(hs, state, gkp, gvp, kcol, decs, keys, values, put):
    for b in range(2):
        rows = block_rows(b)
        loaded = []
        for h in hs:
            last = state[h] * decs[1, h, 0:1, :] if b == 0 else state[h]
            loaded.append(
                (kcol[h, rows, :], keys[h, rows, :], values[h, rows, :], last, gkp[h, rows, :], gvp[h, rows, :])
            )
        done = []
        for scale, key, value, last, part_k, part_v in loaded:
            grad_k = part_k + scale * dot(twice(value), split(last, 1), 1, 1)
            grad_v = part_v + scale * dot(twice(key), split(last, 0), 1, 0)
            done.append((grad_k.astype(BF16), grad_v.astype(BF16)))
        for h, (grad_k, grad_v) in zip(hs, done):
            put(h, rows, grad_k, grad_v)


def first_kernel(
    chips,
    q_hbm,
    k_hbm,
    v_hbm,
    g_hbm,
    gain_ref,
    ld_ref,
    normed_t,
    gq_t,
    gk_h,
    gv_h,
    gkp,
    gvp,
    enter_b,
    kcol,
    decs,
    land,
    qs,
    gs,
    cumr,
    colc,
    ecol,
    att,
    wts,
    s0,
    g0,
    g1,
    gains,
    tx,
    tp,
    tm,
    sb,
    rb,
    pb,
    pin,
    es,
    enter_f,
    zb,
    sqacc,
    pracc,
    in_sem,
    p1s,
    p1r,
    a1s,
    a1r,
    a2s,
    a2r,
    p2s,
    p2r,
    zs,
    zr,
):
    heads, tok = ld_ref.shape
    half = heads // 2
    pairs = half // 2
    zcount = HEAD_TOTAL // heads
    z = lax.axis_index("head")
    d, c, core = one_device_ids(chips)
    partner = (2 * c + 1 - core, z)
    ks, vs = gk_h, gv_h
    enter = (enter_f, enter_b)

    def chip_dev(chip):
        return (2 * chip + core, z)

    sources = (k_hbm, v_hbm, q_hbm, g_hbm)
    by_heads = (ks, vs, qs, gs)

    def load(slot):
        return pltpu.make_async_copy(sources[slot], land.at[slot % 2], in_sem.at[slot])

    for slot in range(2):
        load(slot).start()
    barrier = pltpu.get_barrier_semaphore()
    offsets = far_offsets(chips)
    for o in offsets:
        pl.semaphore_signal(
            barrier, inc=1, device_id=chip_dev(lax.rem(c + o, chips)), device_id_type=MESH
        )
    for i in range(1, zcount):
        pl.semaphore_signal(
            barrier, inc=1, device_id=(d, lax.rem(z + i, zcount)), device_id_type=MESH
        )
    pl.semaphore_signal(barrier, inc=1, device_id=partner, device_id_type=MESH)

    triangle = (
        lax.broadcasted_iota(jnp.int32, (BLOCK, BLOCK), 0)
        <= lax.broadcasted_iota(jnp.int32, (BLOCK, BLOCK), 1)
    ).astype(BF16)
    terms = split3(ld_ref[...]).astype(BF16)
    cums = []
    for b in range(2):
        summed = dot(terms[:, block_rows(b)], triangle, 1, 0)
        cums.append(summed[:heads] + summed[heads : 2 * heads] + summed[2 * heads :])
    ends = [cum[:, BLOCK - 1 :] for cum in cums]
    for b in range(2):
        decay = jnp.broadcast_to(jnp.exp(ends[b]), (heads, HD))
        for h in range(heads):
            decs[b, h] = jnp.broadcast_to(decay[h : h + 1, :], (8, HD))
    for h in range(heads):
        gains[h] = jnp.broadcast_to(gain_ref[h : h + 1, :], (8, HD))

    def columns(x, out):
        padded = jnp.concatenate([split3(x), jnp.zeros((HD - 3 * heads, tok), F32)], axis=0)
        upright = jnp.transpose(padded).astype(BF16)
        term_head = lax.broadcasted_iota(jnp.int32, (HD, 2 * HD), 0) % heads
        lane_head = lax.broadcasted_iota(jnp.int32, (HD, 2 * HD), 1) // HD

        for i in range(heads // 2):
            pick = (term_head == lane_head + 2 * i).astype(F32).astype(BF16)
            both = dot(upright, pick, 1, 0)
            out[2 * i] = both[:, :HD]
            out[2 * i + 1] = both[:, HD:]

    cum = jnp.concatenate(cums, axis=1)
    columns(jnp.concatenate([jnp.exp(e - x) for e, x in zip(ends, cums)], axis=1), kcol)

    def to_heads(slot):
        load(slot).wait()

        def part(i, _):
            at = pl.ds(pl.multiple_of(i * CHUNK, CHUNK), CHUNK)
            by_heads[slot][:, at, :] = pltpu.einshape("thd->htd", land[slot % 2, at])
            return 0

        lax.fori_loop(0, tok // CHUNK, part, 0)

    def to_rows(get, dst):
        def part(i, _):
            at = pl.ds(pl.multiple_of(i * CHUNK, CHUNK), CHUNK)
            dst[at] = pltpu.einshape("htd->thd", get(at))
            return 0

        lax.fori_loop(0, tok // CHUNK, part, 0)

    mask = lax.broadcasted_iota(jnp.int32, (BLOCK, BLOCK), 0) >= lax.broadcasted_iota(
        jnp.int32, (BLOCK, BLOCK), 1
    )

    def decay_table(h, b):
        gap = twice(colc[h, block_rows(b), :]) - cumr[h, 0:1, block_rows(b)]
        return jnp.exp(jnp.where(mask, gap, -jnp.inf))

    def pair1(w, j):
        return pltpu.make_async_remote_copy(
            tx.at[j] if w == 0 else tx.at[j, :HD],
            tp.at[w, j] if w == 0 else tp.at[w, j, :HD],
            p1s.at[w, j],
            p1r.at[w, j],
            device_id=partner,
            device_id_type=MESH,
        )

    def spread1(w, dest, src):
        return pltpu.make_async_remote_copy(
            sb.at[dest] if w == 0 else sb.at[dest, : HD // 2],
            rb.at[w, src] if w == 0 else rb.at[w, src, : HD // 2],
            a1s.at[w, dest],
            a1r.at[w, src],
            device_id=chip_dev(dest),
            device_id_type=MESH,
        )

    def spread2(w, dest, src):
        return pltpu.make_async_remote_copy(
            pb.at[dest],
            pin.at[w, src],
            a2s.at[w, dest],
            a2r.at[w, src],
            device_id=chip_dev(dest),
            device_id_type=MESH,
        )

    def pair2(w, j, owner):
        return pltpu.make_async_remote_copy(
            es.at[j],
            enter[w].at[owner * half + j],
            p2s.at[w, j],
            p2r.at[w, j],
            device_id=partner,
            device_id_type=MESH,
        )

    def begin(w, local_totals):
        first = (core == 0) if w == 0 else (core == 1)

        def one(s, _):
            is_ours = s >= pairs // 2
            i = jnp.where(is_ours, s - pairs // 2, s)
            group = lax.rem(i + c // 8 + 1, pairs // 2)
            js = [4 * group + n for n in range(4)]
            base = jnp.where(is_ours, core, 1 - core) * half
            totals = local_totals([base + j for j in js])
            if w == 0:

                @pl.when(s == 0)
                def _():
                    pl.semaphore_wait(barrier, chips - 1 + 1 + zcount - 1)

            @pl.when(jnp.logical_not(is_ours))
            def _():
                for j, (total, decay) in zip(js, totals):
                    tx[j, :HD] = total
                    if w == 0:
                        tx[j, HD:] = jnp.broadcast_to(decay, (PAD, HD))
                    pair1(w, j).start()

            @pl.when(is_ours)
            def _():
                for j, (total, decay) in zip(js, totals):
                    tm[j, :HD] = total
                    if w == 0:
                        tm[j, HD:] = jnp.broadcast_to(decay, (PAD, HD))
                    pair1(w, j).wait_recv()
                    other = tp[w, j, :HD]
                    other_decay = tp[0, j, HD : HD + 1]
                    chip_total = (
                        jnp.where(first, other_decay, 1.0) * total
                        + jnp.where(first, 1.0, decay) * other
                    )
                    chip_decay = jnp.broadcast_to(decay * other_decay, (PAD, HD))
                    for part in range(2):
                        dest = 2 * j + part
                        sb[dest, : HD // 2] = chip_total[part * (HD // 2) : (part + 1) * (HD // 2)]
                        if w == 0:
                            sb[dest, HD // 2 :] = chip_decay
                for o in (2, 6, 1, 3, 5, 7, 4, 0):
                    dest = len(js) * 2 * group + lax.rem(c + o, len(js) * 2)

                    @pl.when(dest != c)
                    def _():
                        spread1(w, dest, c).start()

            return 0

        lax.fori_loop(0, pairs, one, 0)
        if w == 0:
            rb[w, c] = sb[c]
        else:
            rb[w, c, : HD // 2] = sb[c, : HD // 2]

    def middle(w):
        for o in reversed(offsets):
            src = lax.rem(c + o, chips)
            spread1(w, src, src).wait_recv()
        carried = jnp.zeros((HD // 2, HD), F32)
        for i in range(chips):
            src = i if w == 0 else chips - 1 - i
            pb[src] = carried
            carried = rb[0, src, HD // 2 : HD // 2 + 1] * carried + rb[w, src, : HD // 2]

        for o in offsets:
            spread2(w, lax.rem(c + o, chips), c).start()
        pin[w, c] = pb[c]

    def finish(w):
        first = (core == 0) if w == 0 else (core == 1)

        def ours(i, _):
            j = lax.rem(i + c // 2, half)
            for part in range(2):
                src = 2 * j + part

                @pl.when(src != c)
                def _():
                    spread2(w, src, src).wait_recv()

            entering = jnp.concatenate([pin[w, 2 * j], pin[w, 2 * j + 1]], axis=0)
            decay = jnp.where(first, tm[j, HD : HD + 1], tp[0, j, HD : HD + 1])
            total = jnp.where(first, tm[j, :HD], tp[w, j, :HD])
            after = decay * entering + total
            es[j] = jnp.where(first, after, entering)
            pair2(w, j, core).start()
            enter[w][core * half + j] = jnp.where(first, entering, after)
            return 0

        lax.fori_loop(0, half, ours, 0)

    def drain(w):
        def by_pair(j, _):
            pair1(w, j).wait_send()
            pair2(w, j, core).wait_send()
            return 0

        lax.fori_loop(0, half, by_pair, 0)

        def spreads(i, _):
            dest = lax.rem(c + i, chips)
            spread1(w, dest, c).wait_send()
            spread2(w, dest, c).wait_send()
            return 0

        lax.fori_loop(1, chips, spreads, 0)

    to_heads(0)
    load(2).start()
    to_heads(1)
    load(3).start()

    def key_value(hs):
        loaded = [
            [
                (ks[h, block_rows(b), :], vs[h, block_rows(b), :].astype(F32), kcol[h, block_rows(b), :])
                for b in range(2)
            ]
            for h in hs
        ]
        decays = [(decs[0, h, 0:1, :], decs[1, h, 0:1, :]) for h in hs]
        out = []
        for blocks, (end0, end1) in zip(loaded, decays):
            parts = []
            for key, value, scale in blocks:
                both = dot(key, split(value * scale, 1), 0, 0)
                parts.append(both[:, :HD] + both[:, HD:])
            out.append((end1 * parts[0] + parts[1], end0 * end1, parts[0]))
        for h, (_, _, part) in zip(hs, out):
            s0[h] = part
        return [o[:2] for o in out]

    begin(0, key_value)
    for h in range(heads):
        cumr[h] = jnp.broadcast_to(cum[h : h + 1, :], (8, tok))
    columns(cum, colc)
    columns(jnp.exp(cum), ecol)
    to_heads(2)

    def intra_forward(h, _):
        for b in range(2):
            rows = block_rows(b)
            query = qs[h, rows, :]
            raw = dot(query, ks[h, rows, :], 1, 1)
            weights = (raw * decay_table(h, b)).astype(BF16)
            wts[h, b] = weights
            inner = dot(weights, vs[h, rows, :], 1, 0)
            if b == 1:
                inner = inner + ecol[h, rows, :] * dot(twice(query), split(s0[h], 0), 1, 0)
            att[h, rows, :] = inner
        return 0

    lax.fori_loop(0, EARLY, intra_forward, 0)
    middle(0)
    lax.fori_loop(EARLY, heads, intra_forward, 0)
    to_heads(3)
    sqacc[...] = jnp.zeros_like(sqacc)
    pracc[...] = jnp.zeros_like(pracc)

    def attend(hs, b):
        rows = block_rows(b)
        loaded = []
        for h in hs:
            state = enter_f[h] if b == 0 else enter_f[h] * decs[0, h, 0:1, :]
            loaded.append(
                (
                    qs[h, rows, :],
                    state,
                    ecol[h, rows, :],
                    att[h, rows, :],
                    gains[h, 0:1, :] * gs[h, rows, :].astype(F32),
                )
            )
        squares, products = sqacc[rows, :], pracc[rows, :]
        done = []
        for query, state, scale, inner, scaled in loaded:
            whole = inner + scale * dot(twice(query), split(state, 0), 1, 0)
            squares += whole * whole
            products += scaled * whole
            done.append(whole)
        for h, whole in zip(hs, done):
            att[h, rows, :] = whole
        sqacc[rows, :] = squares
        pracc[rows, :] = products

    def across(b, i):
        return pltpu.make_async_remote_copy(
            zb.at[b, 0],
            zb.at[b, i],
            zs.at[b, i],
            zr.at[b, i],
            device_id=(d, lax.rem(z + i, zcount)),
            device_id_type=MESH,
        )

    finish(0)
    for b in range(2):

        def attend_ours(i, _):
            attend([core * half + 4 * i + n for n in range(4)], b)
            return 0

        def attend_theirs(i, _):
            js = [4 * i + n for n in range(4)]
            if b == 0:
                for j in js:
                    pair2(0, j, 1 - core).wait_recv()
            attend([(1 - core) * half + j for j in js], b)
            return 0

        lax.fori_loop(0, pairs // 2, attend_ours, 0)
        lax.fori_loop(0, pairs // 2, attend_theirs, 0)
        rows = block_rows(b)
        zb[b, 0, 0:1, :] = jnp.sum(jnp.transpose(sqacc[rows, :]), axis=0, keepdims=True)
        zb[b, 0, 1:2, :] = jnp.sum(jnp.transpose(pracc[rows, :]), axis=0, keepdims=True)
        zb[b, 0, 2:, :] = jnp.zeros((6, BLOCK), F32)
        for i in range(1, zcount):
            across(b, i).start()

    def grads(hs, b):
        rows = block_rows(b)
        loaded = [
            (
                gains[h, 0:1, :] * gs[h, rows, :].astype(F32),
                att[h, rows, :],
                ecol[h, rows, :],
                qs[h, rows, :],
            )
            for h in hs
        ]
        inv, shift = sqacc[rows, :], pracc[rows, :]
        out = []
        for scaled, whole, scale, query in loaded:
            grad = ((scaled - whole * shift) * inv).astype(BF16)
            both = dot(query, split(grad.astype(F32) * scale, 1), 0, 0)
            out.append((grad, both[:, :HD] + both[:, HD:]))
        for h, (grad, _) in zip(hs, out):
            gs[h, rows, :] = grad
        return [part for _, part in out]

    def norms(b):
        for i in range(1, zcount):
            across(b, i).wait()
        summed = zb[b, 0]
        for i in range(1, zcount):
            summed = summed + zb[b, i]
        inv_row = lax.rsqrt(summed[0:1, :] / (HEAD_TOTAL * HD) + 1e-06)
        mean_row = summed[1:2, :] * inv_row / (HEAD_TOTAL * HD)
        rows = block_rows(b)
        sqacc[rows, :] = jnp.transpose(jnp.broadcast_to(inv_row, (HD, BLOCK)))
        pracc[rows, :] = jnp.transpose(jnp.broadcast_to(inv_row * mean_row, (HD, BLOCK)))

    norms(0)

    def early_grads(i, _):
        hs = [4 * i + n for n in range(4)]
        for h, part in zip(hs, grads(hs, 0)):
            g0[h] = part
        return 0

    lax.fori_loop(0, heads // 4, early_grads, 0)
    norms(1)

    def late_grads(hs):
        early = [(g0[h], decs[0, h, 0:1, :], decs[1, h, 0:1, :]) for h in hs]
        parts = grads(hs, 1)
        for h, part in zip(hs, parts):
            g1[h] = part
        return [(part0 + end0 * part1, end0 * end1) for (part0, end0, end1), part1 in zip(early, parts)]

    drain(0)
    begin(1, late_grads)

    def intra_backward(h, _):
        enter_h = enter_f[h]
        at_block = (enter_h, decs[0, h, 0:1, :] * enter_h + s0[h])
        for b in range(2):
            rows = block_rows(b)
            grad = gs[h, rows, :]
            key, value = ks[h, rows, :], vs[h, rows, :]
            scores = (dot(grad, value, 1, 1) * decay_table(h, b)).astype(BF16)
            carried = dot(twice(grad), split(at_block[b], 1), 1, 1)
            grad_q = dot(scores, key, 1, 0) + ecol[h, rows, :] * carried
            part_k = dot(scores, qs[h, rows, :], 0, 0)
            qs[h, rows, :] = grad_q.astype(BF16)
            part_v = dot(wts[h, b], grad, 0, 0)
            if b == 0:
                scale = kcol[h, rows, :]
                part_k = part_k + scale * dot(twice(value), split(g1[h], 1), 1, 1)
                part_v = part_v + scale * dot(twice(key), split(g1[h], 0), 1, 0)
            gkp[h, rows, :] = part_k
            gvp[h, rows, :] = part_v
        return 0

    lax.fori_loop(0, half, intra_backward, 0)
    middle(1)
    lax.fori_loop(half, heads, intra_backward, 0)

    def normed_part(at):
        gain = jnp.concatenate([gains[h, 0:1, :] for h in range(heads)], axis=0)
        return (att[:, at, :] * sqacc[at, :][None] * gain[:, None, :]).astype(BF16)

    to_rows(normed_part, normed_t)
    to_rows(lambda at: qs[:, at, :], gq_t)
    finish(1)

    def put(h, rows, grad_k, grad_v):
        gk_h[h, rows, :] = grad_k
        gv_h[h, rows, :] = grad_v

    def close_ours(i, _):
        hs = [core * half + 4 * i + n for n in range(4)]
        close_heads(hs, enter_b, gkp, gvp, kcol, decs, ks, vs, put)
        return 0

    lax.fori_loop(0, pairs // 2, close_ours, 0)

    def arrived(j, _):
        pair2(1, j, 1 - core).wait_recv()
        return 0

    lax.fori_loop(0, half, arrived, 0)
    drain(1)


def second_kernel(
    normed_t,
    gq_t,
    gk_h,
    gv_h,
    gkp,
    gvp,
    enter_b,
    kcol,
    decs,
    normed_hbm,
    gq_hbm,
    gk_hbm,
    gv_hbm,
    done_k,
    done_v,
    land,
    first_sem,
    out_sem,
):
    heads, tok = kcol.shape[0], kcol.shape[1]
    half = heads // 2
    core = lax.rem(lax.axis_index("seq"), 2)
    ready = [
        pltpu.make_async_copy(src, dst, first_sem.at[i])
        for i, (src, dst) in enumerate(((normed_t, normed_hbm), (gq_t, gq_hbm)))
    ]
    for copy in ready:
        copy.start()

    def put(h, rows, grad_k, grad_v):
        done_k[h, rows, :] = grad_k
        done_v[h, rows, :] = grad_v

    def close_theirs(i, _):
        hs = [(1 - core) * half + 4 * i + n for n in range(4)]
        close_heads(hs, enter_b, gkp, gvp, kcol, decs, gk_h, gv_h, put)
        for j in range(4):
            h = core * half + 4 * i + j
            done_k[h] = gk_h[h]
            done_v[h] = gv_h[h]
        return 0

    lax.fori_loop(0, half // 4, close_theirs, 0)
    outs = ((done_k, gk_hbm), (done_v, gv_hbm))

    def out(slot, i):
        at = pl.ds(pl.multiple_of(i * CHUNK, CHUNK), CHUNK)
        return pltpu.make_async_copy(land.at[slot, at], outs[slot][1].at[at], out_sem.at[slot, i])

    for slot in range(2):

        def part(i, _):
            at = pl.ds(pl.multiple_of(i * CHUNK, CHUNK), CHUNK)
            land[slot, at] = pltpu.einshape("htd->thd", outs[slot][0][:, at, :])
            out(slot, i).start()
            return 0

        lax.fori_loop(0, tok // CHUNK, part, 0)
    for slot in range(2):

        def wait(i, _):
            out(slot, i).wait()
            return 0

        lax.fori_loop(0, tok // CHUNK, wait, 0)
    for copy in ready:
        copy.wait()


def on_device(chips, query_rows, key_rows, value_rows, output_grad, norm_gain, log_decay):
    tok, heads, _ = query_rows.shape
    half = heads // 2
    zcount = HEAD_TOTAL // heads
    rows = jax.ShapeDtypeStruct((tok, heads, HD), BF16)
    hbm = pl.BlockSpec(memory_space=pl.ANY)
    vmem = pl.BlockSpec(memory_space=pltpu.VMEM)
    dma = pltpu.SemaphoreType.DMA

    def by_head(dtype):
        return pltpu.VMEM((heads, tok, HD), dtype)

    state = pltpu.VMEM((heads, HD, HD), F32)
    between = (
        pltpu.VMEM((tok, heads, HD), BF16),
        pltpu.VMEM((tok, heads, HD), BF16),
        by_head(BF16),
        by_head(BF16),
        by_head(F32),
        by_head(F32),
        state,
        by_head(F32),
        pltpu.VMEM((2, heads, 8, HD), F32),
    )
    made = pl.pallas_call(
        functools.partial(first_kernel, chips),
        out_shape=between,
        in_specs=[hbm] * 4 + [vmem] * 2,
        out_specs=[vmem] * len(between),
        scratch_shapes=[
            pltpu.VMEM((2, tok, heads, HD), BF16),
            by_head(BF16),
            by_head(BF16),
            pltpu.VMEM((heads, 8, tok), F32),
            by_head(F32),
            by_head(F32),
            by_head(F32),
            pltpu.VMEM((heads, tok // BLOCK, BLOCK, BLOCK), BF16),
            state,
            state,
            state,
            pltpu.VMEM((heads, 8, HD), F32),
            pltpu.VMEM((half, HD + PAD, HD), F32),
            pltpu.VMEM((2, half, HD + PAD, HD), F32),
            pltpu.VMEM((half, HD + PAD, HD), F32),
            pltpu.VMEM((chips, HD // 2 + PAD, HD), F32),
            pltpu.VMEM((2, chips, HD // 2 + PAD, HD), F32),
            pltpu.VMEM((chips, HD // 2, HD), F32),
            pltpu.VMEM((2, chips, HD // 2, HD), F32),
            pltpu.VMEM((half, HD, HD), F32),
            state,
            pltpu.VMEM((2, zcount, 8, BLOCK), F32),
            pltpu.VMEM((tok, HD), F32),
            pltpu.VMEM((tok, HD), F32),
            dma((4,)),
            dma((2, half)),
            dma((2, half)),
            dma((2, chips)),
            dma((2, chips)),
            dma((2, chips)),
            dma((2, chips)),
            dma((2, half)),
            dma((2, half)),
            dma((2, zcount)),
            dma((2, zcount)),
        ],
        compiler_params=pltpu.CompilerParams(
            collective_id=0, has_side_effects=True, vmem_limit_bytes=FIRST_VMEM
        ),
        cost_estimate=pl.CostEstimate(
            flops=2 * 10**10, bytes_accessed=8 << 20, transcendentals=10**7
        ),
    )(query_rows, key_rows, value_rows, output_grad, norm_gain, log_decay)
    made = [pltpu.with_memory_space_constraint(m, pltpu.VMEM) for m in made]
    return pl.pallas_call(
        second_kernel,
        out_shape=(rows,) * 4,
        in_specs=[vmem] * len(between),
        out_specs=[hbm] * 4,
        scratch_shapes=[
            by_head(BF16),
            by_head(BF16),
            pltpu.VMEM((2, tok, heads, HD), BF16),
            dma((2,)),
            dma((2, tok // CHUNK)),
        ],
        compiler_params=pltpu.CompilerParams(vmem_limit_bytes=SECOND_VMEM),
        cost_estimate=pl.CostEstimate(
            flops=2 * 10**9, bytes_accessed=8 << 20, transcendentals=10**6
        ),
    )(*made)


def solution(mesh):
    rows = P("seq", "head", None)
    return jax.shard_map(
        functools.partial(on_device, mesh.shape["seq"] // 2),
        mesh=mesh,
        in_specs=(rows, rows, rows, rows, P("head", None), P("head", "seq")),
        out_specs=(rows,) * 4,
        check_vma=False,
    )
```

```python
import functools

import jax
import jax.numpy as jnp
from jax import lax
from jax.experimental import pallas as pl
from jax.experimental.pallas import tpu as pltpu
from jax.sharding import PartitionSpec as P

HEAD_TOTAL = 64
HD = 128
BLOCK = 256
CHUNK = 64
PAD = 8
EARLY = 6
FIRST_VMEM = 38 << 20
SECOND_VMEM = 14 << 20
MESH = pl.DeviceIdType.MESH
F32 = jnp.float32
BF16 = jnp.bfloat16


def dot(a, b, ca, cb):
    return lax.dot_general(a, b, (((ca,), (cb,)), ((), ())), preferred_element_type=F32)


def split(x, axis):
    hi = x.astype(BF16)
    lo = (x - hi.astype(F32)).astype(BF16)
    return jnp.concatenate([hi, lo], axis=axis)


def split3(x):
    hi = x.astype(BF16).astype(F32)
    mid = (x - hi).astype(BF16).astype(F32)
    lo = (x - hi - mid).astype(BF16).astype(F32)
    return jnp.concatenate([hi, mid, lo], axis=0)


def far_offsets(chips):
    side = int(chips**0.5)

    def hops(o):
        return sum(min(n, side - n) for n in divmod(o, side))

    return sorted(range(1, chips), key=lambda o: (-hops(o), o))


def twice(x):
    return jnp.concatenate([x, x], axis=1)


def one_device_ids(chips):
    d = lax.axis_index("seq")
    c = d // 2
    return d, c, d - 2 * c


def block_rows(b):
    return slice(b * BLOCK, (b + 1) * BLOCK)


def close_heads(hs, state, gkp, gvp, kcol, decs, keys, values, put):
    for b in range(2):
        rows = block_rows(b)
        loaded = []
        for h in hs:
            last = state[h] * decs[1, h, 0:1, :] if b == 0 else state[h]
            loaded.append(
                (kcol[h, rows, :], keys[h, rows, :], values[h, rows, :], last, gkp[h, rows, :], gvp[h, rows, :])
            )
        done = []
        for scale, key, value, last, part_k, part_v in loaded:
            grad_k = part_k + scale * dot(twice(value), split(last, 1), 1, 1)
            grad_v = part_v + scale * dot(twice(key), split(last, 0), 1, 0)
            done.append((grad_k.astype(BF16), grad_v.astype(BF16)))
        for h, (grad_k, grad_v) in zip(hs, done):
            put(h, rows, grad_k, grad_v)


def first_kernel(
    chips,
    q_hbm,
    k_hbm,
    v_hbm,
    g_hbm,
    gain_ref,
    ld_ref,
    normed_t,
    gq_t,
    gk_h,
    gv_h,
    gkp,
    gvp,
    enter_b,
    kcol,
    decs,
    land,
    qs,
    gs,
    cumr,
    colc,
    ecol,
    att,
    wts,
    s0,
    g0,
    g1,
    gains,
    tx,
    tp,
    tm,
    sb,
    rb,
    pb,
    pin,
    es,
    enter_f,
    zb,
    sqacc,
    pracc,
    in_sem,
    p1s,
    p1r,
    a1s,
    a1r,
    a2s,
    a2r,
    p2s,
    p2r,
    zs,
    zr,
):
    heads, tok = ld_ref.shape
    half = heads // 2
    pairs = half // 2
    zcount = HEAD_TOTAL // heads
    z = lax.axis_index("head")
    d, c, core = one_device_ids(chips)
    partner = (2 * c + 1 - core, z)
    ks, vs = gk_h, gv_h
    enter = (enter_f, enter_b)

    def chip_dev(chip):
        return (2 * chip + core, z)

    sources = (k_hbm, v_hbm, q_hbm, g_hbm)
    by_heads = (ks, vs, qs, gs)

    def load(slot):
        return pltpu.make_async_copy(sources[slot], land.at[slot % 2], in_sem.at[slot])

    for slot in range(2):
        load(slot).start()
    barrier = pltpu.get_barrier_semaphore()
    offsets = far_offsets(chips)
    for o in offsets:
        pl.semaphore_signal(
            barrier, inc=1, device_id=chip_dev(lax.rem(c + o, chips)), device_id_type=MESH
        )
    for i in range(1, zcount):
        pl.semaphore_signal(
            barrier, inc=1, device_id=(d, lax.rem(z + i, zcount)), device_id_type=MESH
        )
    pl.semaphore_signal(barrier, inc=1, device_id=partner, device_id_type=MESH)

    triangle = (
        lax.broadcasted_iota(jnp.int32, (BLOCK, BLOCK), 0)
        <= lax.broadcasted_iota(jnp.int32, (BLOCK, BLOCK), 1)
    ).astype(BF16)
    terms = split3(ld_ref[...]).astype(BF16)
    cums = []
    for b in range(2):
        summed = dot(terms[:, block_rows(b)], triangle, 1, 0)
        cums.append(summed[:heads] + summed[heads : 2 * heads] + summed[2 * heads :])
    ends = [cum[:, BLOCK - 1 :] for cum in cums]
    for b in range(2):
        decay = jnp.broadcast_to(jnp.exp(ends[b]), (heads, HD))
        for h in range(heads):
            decs[b, h] = jnp.broadcast_to(decay[h : h + 1, :], (8, HD))
    for h in range(heads):
        gains[h] = jnp.broadcast_to(gain_ref[h : h + 1, :], (8, HD))

    def columns(x, out):
        padded = jnp.concatenate([split3(x), jnp.zeros((HD - 3 * heads, tok), F32)], axis=0)
        upright = jnp.transpose(padded).astype(BF16)
        term_head = lax.broadcasted_iota(jnp.int32, (HD, 2 * HD), 0) % heads
        lane_head = lax.broadcasted_iota(jnp.int32, (HD, 2 * HD), 1) // HD

        for i in range(heads // 2):
            pick = (term_head == lane_head + 2 * i).astype(F32).astype(BF16)
            both = dot(upright, pick, 1, 0)
            out[2 * i] = both[:, :HD]
            out[2 * i + 1] = both[:, HD:]

    cum = jnp.concatenate(cums, axis=1)
    columns(jnp.concatenate([jnp.exp(e - x) for e, x in zip(ends, cums)], axis=1), kcol)

    def to_heads(slot):
        load(slot).wait()

        def part(i, _):
            at = pl.ds(pl.multiple_of(i * CHUNK, CHUNK), CHUNK)
            by_heads[slot][:, at, :] = pltpu.einshape("thd->htd", land[slot % 2, at])
            return 0

        lax.fori_loop(0, tok // CHUNK, part, 0)

    def to_rows(get, dst):
        def part(i, _):
            at = pl.ds(pl.multiple_of(i * CHUNK, CHUNK), CHUNK)
            dst[at] = pltpu.einshape("htd->thd", get(at))
            return 0

        lax.fori_loop(0, tok // CHUNK, part, 0)

    mask = lax.broadcasted_iota(jnp.int32, (BLOCK, BLOCK), 0) >= lax.broadcasted_iota(
        jnp.int32, (BLOCK, BLOCK), 1
    )

    def decay_table(h, b):
        gap = twice(colc[h, block_rows(b), :]) - cumr[h, 0:1, block_rows(b)]
        return jnp.exp(jnp.where(mask, gap, -jnp.inf))

    def pair1(w, j):
        return pltpu.make_async_remote_copy(
            tx.at[j] if w == 0 else tx.at[j, :HD],
            tp.at[w, j] if w == 0 else tp.at[w, j, :HD],
            p1s.at[w, j],
            p1r.at[w, j],
            device_id=partner,
            device_id_type=MESH,
        )

    def spread1(w, dest, src):
        return pltpu.make_async_remote_copy(
            sb.at[dest] if w == 0 else sb.at[dest, : HD // 2],
            rb.at[w, src] if w == 0 else rb.at[w, src, : HD // 2],
            a1s.at[w, dest],
            a1r.at[w, src],
            device_id=chip_dev(dest),
            device_id_type=MESH,
        )

    def spread2(w, dest, src):
        return pltpu.make_async_remote_copy(
            pb.at[dest],
            pin.at[w, src],
            a2s.at[w, dest],
            a2r.at[w, src],
            device_id=chip_dev(dest),
            device_id_type=MESH,
        )

    def pair2(w, j, owner):
        return pltpu.make_async_remote_copy(
            es.at[j],
            enter[w].at[owner * half + j],
            p2s.at[w, j],
            p2r.at[w, j],
            device_id=partner,
            device_id_type=MESH,
        )

    def begin(w, local_totals):
        first = (core == 0) if w == 0 else (core == 1)

        def one(s, _):
            is_ours = s >= pairs // 2
            i = jnp.where(is_ours, s - pairs // 2, s)
            group = lax.rem(i + c // 8 + 1, pairs // 2)
            js = [4 * group + n for n in range(4)]
            base = jnp.where(is_ours, core, 1 - core) * half
            totals = local_totals([base + j for j in js])
            if w == 0:

                @pl.when(s == 0)
                def _():
                    pl.semaphore_wait(barrier, chips - 1 + 1 + zcount - 1)

            @pl.when(jnp.logical_not(is_ours))
            def _():
                for j, (total, decay) in zip(js, totals):
                    tx[j, :HD] = total
                    if w == 0:
                        tx[j, HD:] = jnp.broadcast_to(decay, (PAD, HD))
                    pair1(w, j).start()

            @pl.when(is_ours)
            def _():
                for j, (total, decay) in zip(js, totals):
                    tm[j, :HD] = total
                    if w == 0:
                        tm[j, HD:] = jnp.broadcast_to(decay, (PAD, HD))
                    pair1(w, j).wait_recv()
                    other = tp[w, j, :HD]
                    other_decay = tp[0, j, HD : HD + 1]
                    chip_total = (
                        jnp.where(first, other_decay, 1.0) * total
                        + jnp.where(first, 1.0, decay) * other
                    )
                    chip_decay = jnp.broadcast_to(decay * other_decay, (PAD, HD))
                    for part in range(2):
                        dest = 2 * j + part
                        sb[dest, : HD // 2] = chip_total[part * (HD // 2) : (part + 1) * (HD // 2)]
                        if w == 0:
                            sb[dest, HD // 2 :] = chip_decay
                for fx, fy in ((0, 2), (0, 1), (0, 3), (1, 2), (0, 0), (1, 1), (1, 3), (1, 0)):
                    column = lax.rem(c // 4 + fx + i, 2)
                    dest = len(js) * 2 * group + 4 * column + lax.rem(c + fy, 4)

                    @pl.when(dest != c)
                    def _():
                        spread1(w, dest, c).start()

            return 0

        lax.fori_loop(0, pairs, one, 0)
        if w == 0:
            rb[w, c] = sb[c]
        else:
            rb[w, c, : HD // 2] = sb[c, : HD // 2]

    def middle(w):
        for o in reversed(offsets):
            src = lax.rem(c + o, chips)
            spread1(w, src, src).wait_recv()
        carried = jnp.zeros((HD // 2, HD), F32)
        for i in range(chips):
            src = i if w == 0 else chips - 1 - i
            pb[src] = carried
            carried = rb[0, src, HD // 2 : HD // 2 + 1] * carried + rb[w, src, : HD // 2]

        for o in offsets:
            spread2(w, lax.rem(c + o, chips), c).start()
        pin[w, c] = pb[c]

    def finish(w):
        first = (core == 0) if w == 0 else (core == 1)

        def ours(i, _):
            j = lax.rem(i + c // 2, half)
            for part in range(2):
                src = 2 * j + part

                @pl.when(src != c)
                def _():
                    spread2(w, src, src).wait_recv()

            entering = jnp.concatenate([pin[w, 2 * j], pin[w, 2 * j + 1]], axis=0)
            decay = jnp.where(first, tm[j, HD : HD + 1], tp[0, j, HD : HD + 1])
            total = jnp.where(first, tm[j, :HD], tp[w, j, :HD])
            after = decay * entering + total
            es[j] = jnp.where(first, after, entering)
            pair2(w, j, core).start()
            enter[w][core * half + j] = jnp.where(first, entering, after)
            return 0

        lax.fori_loop(0, half, ours, 0)

    def drain(w):
        def by_pair(j, _):
            pair1(w, j).wait_send()
            pair2(w, j, core).wait_send()
            return 0

        lax.fori_loop(0, half, by_pair, 0)

        def spreads(i, _):
            dest = lax.rem(c + i, chips)
            spread1(w, dest, c).wait_send()
            spread2(w, dest, c).wait_send()
            return 0

        lax.fori_loop(1, chips, spreads, 0)

    to_heads(0)
    load(2).start()
    to_heads(1)
    load(3).start()

    def key_value(hs):
        loaded = [
            [
                (ks[h, block_rows(b), :], vs[h, block_rows(b), :].astype(F32), kcol[h, block_rows(b), :])
                for b in range(2)
            ]
            for h in hs
        ]
        decays = [(decs[0, h, 0:1, :], decs[1, h, 0:1, :]) for h in hs]
        out = []
        for blocks, (end0, end1) in zip(loaded, decays):
            parts = []
            for key, value, scale in blocks:
                both = dot(key, split(value * scale, 1), 0, 0)
                parts.append(both[:, :HD] + both[:, HD:])
            out.append((end1 * parts[0] + parts[1], end0 * end1, parts[0]))
        for h, (_, _, part) in zip(hs, out):
            s0[h] = part
        return [o[:2] for o in out]

    begin(0, key_value)
    for h in range(heads):
        cumr[h] = jnp.broadcast_to(cum[h : h + 1, :], (8, tok))
    columns(cum, colc)
    columns(jnp.exp(cum), ecol)
    to_heads(2)

    def intra_forward(h, _):
        for b in range(2):
            rows = block_rows(b)
            query = qs[h, rows, :]
            raw = dot(query, ks[h, rows, :], 1, 1)
            weights = (raw * decay_table(h, b)).astype(BF16)
            wts[h, b] = weights
            inner = dot(weights, vs[h, rows, :], 1, 0)
            if b == 1:
                inner = inner + ecol[h, rows, :] * dot(twice(query), split(s0[h], 0), 1, 0)
            att[h, rows, :] = inner
        return 0

    lax.fori_loop(0, EARLY, intra_forward, 0)
    middle(0)
    lax.fori_loop(EARLY, heads, intra_forward, 0)
    to_heads(3)
    sqacc[...] = jnp.zeros_like(sqacc)
    pracc[...] = jnp.zeros_like(pracc)

    def attend(hs, b):
        rows = block_rows(b)
        loaded = []
        for h in hs:
            state = enter_f[h] if b == 0 else enter_f[h] * decs[0, h, 0:1, :]
            loaded.append(
                (
                    qs[h, rows, :],
                    state,
                    ecol[h, rows, :],
                    att[h, rows, :],
                    gains[h, 0:1, :] * gs[h, rows, :].astype(F32),
                )
            )
        squares, products = sqacc[rows, :], pracc[rows, :]
        done = []
        for query, state, scale, inner, scaled in loaded:
            whole = inner + scale * dot(twice(query), split(state, 0), 1, 0)
            squares += whole * whole
            products += scaled * whole
            done.append(whole)
        for h, whole in zip(hs, done):
            att[h, rows, :] = whole
        sqacc[rows, :] = squares
        pracc[rows, :] = products

    def across(b, i):
        return pltpu.make_async_remote_copy(
            zb.at[b, 0],
            zb.at[b, i],
            zs.at[b, i],
            zr.at[b, i],
            device_id=(d, lax.rem(z + i, zcount)),
            device_id_type=MESH,
        )

    finish(0)
    for b in range(2):

        def attend_ours(i, _):
            attend([core * half + 4 * i + n for n in range(4)], b)
            return 0

        def attend_theirs(i, _):
            js = [4 * i + n for n in range(4)]
            if b == 0:
                for j in js:
                    pair2(0, j, 1 - core).wait_recv()
            attend([(1 - core) * half + j for j in js], b)
            return 0

        lax.fori_loop(0, pairs // 2, attend_ours, 0)
        lax.fori_loop(0, pairs // 2, attend_theirs, 0)
        rows = block_rows(b)
        zb[b, 0, 0:1, :] = jnp.sum(jnp.transpose(sqacc[rows, :]), axis=0, keepdims=True)
        zb[b, 0, 1:2, :] = jnp.sum(jnp.transpose(pracc[rows, :]), axis=0, keepdims=True)
        zb[b, 0, 2:, :] = jnp.zeros((6, BLOCK), F32)
        for i in range(1, zcount):
            across(b, i).start()

    def grads(hs, b):
        rows = block_rows(b)
        loaded = [
            (
                gains[h, 0:1, :] * gs[h, rows, :].astype(F32),
                att[h, rows, :],
                ecol[h, rows, :],
                qs[h, rows, :],
            )
            for h in hs
        ]
        inv, shift = sqacc[rows, :], pracc[rows, :]
        out = []
        for scaled, whole, scale, query in loaded:
            grad = ((scaled - whole * shift) * inv).astype(BF16)
            both = dot(query, split(grad.astype(F32) * scale, 1), 0, 0)
            out.append((grad, both[:, :HD] + both[:, HD:]))
        for h, (grad, _) in zip(hs, out):
            gs[h, rows, :] = grad
        return [part for _, part in out]

    def norms(b):
        for i in range(1, zcount):
            across(b, i).wait()
        summed = zb[b, 0]
        for i in range(1, zcount):
            summed = summed + zb[b, i]
        inv_row = lax.rsqrt(summed[0:1, :] / (HEAD_TOTAL * HD) + 1e-06)
        mean_row = summed[1:2, :] * inv_row / (HEAD_TOTAL * HD)
        rows = block_rows(b)
        sqacc[rows, :] = jnp.transpose(jnp.broadcast_to(inv_row, (HD, BLOCK)))
        pracc[rows, :] = jnp.transpose(jnp.broadcast_to(inv_row * mean_row, (HD, BLOCK)))

    norms(0)

    def early_grads(i, _):
        hs = [4 * i + n for n in range(4)]
        for h, part in zip(hs, grads(hs, 0)):
            g0[h] = part
        return 0

    lax.fori_loop(0, heads // 4, early_grads, 0)
    norms(1)

    def late_grads(hs):
        early = [(g0[h], decs[0, h, 0:1, :], decs[1, h, 0:1, :]) for h in hs]
        parts = grads(hs, 1)
        for h, part in zip(hs, parts):
            g1[h] = part
        return [(part0 + end0 * part1, end0 * end1) for (part0, end0, end1), part1 in zip(early, parts)]

    drain(0)
    begin(1, late_grads)

    def intra_backward(h, _):
        enter_h = enter_f[h]
        at_block = (enter_h, decs[0, h, 0:1, :] * enter_h + s0[h])
        for b in range(2):
            rows = block_rows(b)
            grad = gs[h, rows, :]
            key, value = ks[h, rows, :], vs[h, rows, :]
            scores = (dot(grad, value, 1, 1) * decay_table(h, b)).astype(BF16)
            carried = dot(twice(grad), split(at_block[b], 1), 1, 1)
            grad_q = dot(scores, key, 1, 0) + ecol[h, rows, :] * carried
            part_k = dot(scores, qs[h, rows, :], 0, 0)
            qs[h, rows, :] = grad_q.astype(BF16)
            part_v = dot(wts[h, b], grad, 0, 0)
            if b == 0:
                scale = kcol[h, rows, :]
                part_k = part_k + scale * dot(twice(value), split(g1[h], 1), 1, 1)
                part_v = part_v + scale * dot(twice(key), split(g1[h], 0), 1, 0)
            gkp[h, rows, :] = part_k
            gvp[h, rows, :] = part_v
        return 0

    lax.fori_loop(0, half, intra_backward, 0)
    middle(1)
    lax.fori_loop(half, heads, intra_backward, 0)

    def normed_part(at):
        gain = jnp.concatenate([gains[h, 0:1, :] for h in range(heads)], axis=0)
        return (att[:, at, :] * sqacc[at, :][None] * gain[:, None, :]).astype(BF16)

    to_rows(normed_part, normed_t)
    to_rows(lambda at: qs[:, at, :], gq_t)
    finish(1)

    def put(h, rows, grad_k, grad_v):
        gk_h[h, rows, :] = grad_k
        gv_h[h, rows, :] = grad_v

    def close_ours(i, _):
        hs = [core * half + 4 * i + n for n in range(4)]
        close_heads(hs, enter_b, gkp, gvp, kcol, decs, ks, vs, put)
        return 0

    lax.fori_loop(0, pairs // 2, close_ours, 0)

    def arrived(j, _):
        pair2(1, j, 1 - core).wait_recv()
        return 0

    lax.fori_loop(0, half, arrived, 0)
    drain(1)


def second_kernel(
    normed_t,
    gq_t,
    gk_h,
    gv_h,
    gkp,
    gvp,
    enter_b,
    kcol,
    decs,
    normed_hbm,
    gq_hbm,
    gk_hbm,
    gv_hbm,
    done_k,
    done_v,
    land,
    first_sem,
    out_sem,
):
    heads, tok = kcol.shape[0], kcol.shape[1]
    half = heads // 2
    core = lax.rem(lax.axis_index("seq"), 2)
    ready = [
        pltpu.make_async_copy(src, dst, first_sem.at[i])
        for i, (src, dst) in enumerate(((normed_t, normed_hbm), (gq_t, gq_hbm)))
    ]
    for copy in ready:
        copy.start()

    def put(h, rows, grad_k, grad_v):
        done_k[h, rows, :] = grad_k
        done_v[h, rows, :] = grad_v

    def close_theirs(i, _):
        hs = [(1 - core) * half + 4 * i + n for n in range(4)]
        close_heads(hs, enter_b, gkp, gvp, kcol, decs, gk_h, gv_h, put)
        for j in range(4):
            h = core * half + 4 * i + j
            done_k[h] = gk_h[h]
            done_v[h] = gv_h[h]
        return 0

    lax.fori_loop(0, half // 4, close_theirs, 0)
    outs = ((done_k, gk_hbm), (done_v, gv_hbm))

    def out(slot, i):
        at = pl.ds(pl.multiple_of(i * CHUNK, CHUNK), CHUNK)
        return pltpu.make_async_copy(land.at[slot, at], outs[slot][1].at[at], out_sem.at[slot, i])

    for slot in range(2):

        def part(i, _):
            at = pl.ds(pl.multiple_of(i * CHUNK, CHUNK), CHUNK)
            land[slot, at] = pltpu.einshape("htd->thd", outs[slot][0][:, at, :])
            out(slot, i).start()
            return 0

        lax.fori_loop(0, tok // CHUNK, part, 0)
    for slot in range(2):

        def wait(i, _):
            out(slot, i).wait()
            return 0

        lax.fori_loop(0, tok // CHUNK, wait, 0)
    for copy in ready:
        copy.wait()


def on_device(chips, query_rows, key_rows, value_rows, output_grad, norm_gain, log_decay):
    tok, heads, _ = query_rows.shape
    half = heads // 2
    zcount = HEAD_TOTAL // heads
    rows = jax.ShapeDtypeStruct((tok, heads, HD), BF16)
    hbm = pl.BlockSpec(memory_space=pl.ANY)
    vmem = pl.BlockSpec(memory_space=pltpu.VMEM)
    dma = pltpu.SemaphoreType.DMA

    def by_head(dtype):
        return pltpu.VMEM((heads, tok, HD), dtype)

    state = pltpu.VMEM((heads, HD, HD), F32)
    between = (
        pltpu.VMEM((tok, heads, HD), BF16),
        pltpu.VMEM((tok, heads, HD), BF16),
        by_head(BF16),
        by_head(BF16),
        by_head(F32),
        by_head(F32),
        state,
        by_head(F32),
        pltpu.VMEM((2, heads, 8, HD), F32),
    )
    made = pl.pallas_call(
        functools.partial(first_kernel, chips),
        out_shape=between,
        in_specs=[hbm] * 4 + [vmem] * 2,
        out_specs=[vmem] * len(between),
        scratch_shapes=[
            pltpu.VMEM((2, tok, heads, HD), BF16),
            by_head(BF16),
            by_head(BF16),
            pltpu.VMEM((heads, 8, tok), F32),
            by_head(F32),
            by_head(F32),
            by_head(F32),
            pltpu.VMEM((heads, tok // BLOCK, BLOCK, BLOCK), BF16),
            state,
            state,
            state,
            pltpu.VMEM((heads, 8, HD), F32),
            pltpu.VMEM((half, HD + PAD, HD), F32),
            pltpu.VMEM((2, half, HD + PAD, HD), F32),
            pltpu.VMEM((half, HD + PAD, HD), F32),
            pltpu.VMEM((chips, HD // 2 + PAD, HD), F32),
            pltpu.VMEM((2, chips, HD // 2 + PAD, HD), F32),
            pltpu.VMEM((chips, HD // 2, HD), F32),
            pltpu.VMEM((2, chips, HD // 2, HD), F32),
            pltpu.VMEM((half, HD, HD), F32),
            state,
            pltpu.VMEM((2, zcount, 8, BLOCK), F32),
            pltpu.VMEM((tok, HD), F32),
            pltpu.VMEM((tok, HD), F32),
            dma((4,)),
            dma((2, half)),
            dma((2, half)),
            dma((2, chips)),
            dma((2, chips)),
            dma((2, chips)),
            dma((2, chips)),
            dma((2, half)),
            dma((2, half)),
            dma((2, zcount)),
            dma((2, zcount)),
        ],
        compiler_params=pltpu.CompilerParams(
            collective_id=0, has_side_effects=True, vmem_limit_bytes=FIRST_VMEM
        ),
        cost_estimate=pl.CostEstimate(
            flops=2 * 10**10, bytes_accessed=8 << 20, transcendentals=10**7
        ),
    )(query_rows, key_rows, value_rows, output_grad, norm_gain, log_decay)
    made = [pltpu.with_memory_space_constraint(m, pltpu.VMEM) for m in made]
    return pl.pallas_call(
        second_kernel,
        out_shape=(rows,) * 4,
        in_specs=[vmem] * len(between),
        out_specs=[hbm] * 4,
        scratch_shapes=[
            by_head(BF16),
            by_head(BF16),
            pltpu.VMEM((2, tok, heads, HD), BF16),
            dma((2,)),
            dma((2, tok // CHUNK)),
        ],
        compiler_params=pltpu.CompilerParams(vmem_limit_bytes=SECOND_VMEM),
        cost_estimate=pl.CostEstimate(
            flops=2 * 10**9, bytes_accessed=8 << 20, transcendentals=10**6
        ),
    )(*made)


def solution(mesh):
    rows = P("seq", "head", None)
    return jax.shard_map(
        functools.partial(on_device, mesh.shape["seq"] // 2),
        mesh=mesh,
        in_specs=(rows, rows, rows, rows, P("head", None), P("head", "seq")),
        out_specs=(rows,) * 4,
        check_vma=False,
    )
```
